512 devices in a mesh: dp: 4 (over x), tensor: 128 (over z, y, core).
Axes of the slice: x: 4, y: 8, z: 8, core: 2. Of those that a mesh axis runs over, the one named last changes fastest.
Arguments:
- hidden: bfloat16 [1024, 4096], P(('dp', 'tensor')), parts along dimension 0, may hold values from -16 to 16
- norm_gain: bfloat16 [4096], replicated, may hold values from 0.5 to 1.5
- head_weight: bfloat16 [65536, 4096], P('tensor'), may hold values from -4 to 4
- gate_up: bfloat16 [2, 28672, 1024], P(None, 'tensor', 'dp'), parts along dimension 2, may hold values from -6 to 6
- targets: int32 [1024], P('dp'), parts along dimension 0, may hold values from 0 to 65535
- doc_ids: int32 [1024], P('dp'), parts along dimension 0, may hold values from 0 to 7, never falling along the last dimension, each value on 1 to 64 neighbouring positions
- vocab_codes: int32 [65536], P('tensor'), may hold values from 0 to 127
- hidden_codes: int32 [28672], P('tensor'), may hold values from 0 to 127
- model_codes: int32 [2, 4096], replicated, may hold values from 0 to 127
Outputs:
- resid_grad: bfloat16 [1024, 4096], P(('dp', 'tensor')), parts along dimension 0
- head_features: float32 [32, 4096], P('dp', 'tensor'), parts along dimension 0
- down_features: float32 [32, 4096], P('dp', 'tensor'), parts along dimension 0
The draws below stay inside these ranges and needn't reach their ends.
There are 4 independent parts, one for each index of `dp`. The reference program is written for one: setup_inputs(seed, part) draws one part's arguments, and reference() takes and returns one part's arrays. A program takes and returns all parts, laid end to end along the dimension named above; an argument that names none is the same for every part. Nothing has to cross between parts.
Inputs may be any that keep to these rules, and one draw needn't show every extreme that they name: `doc_ids`: document ids never fall along the tokens; a document has at most 64 tokens.
All inputs are finite; a program needn't handle non-finite values.
Results may differ from the reference program's by a relative error of at most 0.0033.
Values may be sent and summed in bfloat16 or wider, within the bound.
No kernel may reach another device: no remote copies, remote signals or barrier semaphores. Data moves between devices by JAX's collectives and lax.ppermute only.
A program may use at most 64 MiB of HBM per device.

```python
import math
import jax
import jax.numpy as jnp
import numpy as np
from jax import lax

D = 4096
RANK = 64
DOCS = 8
TOKENS = 256
VOCAB = 65536
FF = 28672


def plant_pattern(width):
    index = jnp.arange(width, dtype=jnp.int32)
    return jnp.where((index + index // 5) % 2 == 0, 1.0, -1.0).astype(jnp.float32)


def draw_head_weight(key, part):
    key = jax.random.fold_in(key, 11)
    row_key, magnitude_key, picking_key = jax.random.split(key, 3)
    sigma = (D // 9) ** (-0.5)
    base = jnp.clip(jax.random.normal(row_key, (VOCAB, D), jnp.float32), -6.0, 6.0) * sigma
    picked = jax.random.permutation(picking_key, VOCAB)[:3]
    magnitude = jax.random.uniform(magnitude_key, (3, D), jnp.float32, 0.5, 1.5)
    planted = magnitude * plant_pattern(D)[None, :] * (333.0 / D)
    return base.at[picked].set(planted).astype(jnp.bfloat16)


def draw_hidden(key, part):
    key = jax.random.fold_in(key, 23)
    noise_key, magnitude_key, picking_key = jax.random.split(key, 3)
    unit_noise = jnp.clip(jax.random.normal(noise_key, (TOKENS, D), jnp.float32), -6.0, 6.0)
    strengths = jnp.array([1.0, 0.6, 0.3, 0.15], jnp.float32)[:, None]
    chosen = jax.random.permutation(picking_key, TOKENS)[:4]
    aligned = jax.random.uniform(magnitude_key, (4, D), jnp.float32, 0.5, 1.5) * plant_pattern(D)[None, :]
    mixed = strengths * aligned + (1.0 - strengths) * unit_noise[chosen]
    scaled = unit_noise
    return scaled.at[chosen].set(mixed).astype(jnp.bfloat16)


def place_ends(entries, own_key, smallest, largest):
    place = [jax.random.randint(jax.random.fold_in(own_key, axis), (), 0, length) for axis, length in enumerate(entries.shape)]
    longest = entries.shape.index(max(entries.shape))
    neighbour = place[:longest] + [(place[longest] + 1) % entries.shape[longest]] + place[longest + 1:]
    return entries.at[tuple(place)].set(smallest).at[tuple(neighbour)].set(largest)


def block_scale(stream_key, extent, cuts, low, top_value):
    loudness, own = 1.0, jax.random.fold_in(stream_key, 6)
    for dim, blocks in cuts:
        draws = jnp.exp(jax.random.uniform(jax.random.fold_in(own, dim), (blocks,), jnp.float32, low / len(cuts), top_value / len(cuts)))
        loudness = loudness * jnp.repeat(draws, extent[dim] // blocks).reshape([-1 if axis == dim else 1 for axis in range(len(extent))])
    return loudness


def split_up(amount, total, bound, lean):
    portions = [(1 << 20) // math.isqrt(grade ** lean) + 1 for grade in range(2, amount + 1)]
    surplus, counts = total - bound - (amount - 1), [1] * (amount - 1)
    while surplus > 0:
        movable = [i for i in range(amount - 1) if counts[i] < bound]
        mass, left = sum([portions[i] for i in movable]), surplus
        for i in movable:
            extra = min(bound - counts[i], max(1, left * portions[i] // mass), surplus)
            counts[i] = counts[i] + extra
            surplus = surplus - extra
    return np.array([bound] + counts)


def uneven(rng, number_of, total, bound, lean):
    if number_of == 2:
        one = jax.random.randint(rng, (), max(1, total - bound), min(bound, total - 1) + 1)
        return jnp.stack([one, total - one])
    lengths = jnp.asarray(split_up(number_of, total, bound, lean), jnp.int32)
    couples = (number_of - 1) // 2
    source_of, taker = lengths[1:1 + 2 * couples:2], lengths[2:2 + 2 * couples:2]
    margin = jnp.minimum(source_of - 1, bound - taker)
    passed = jax.random.randint(jax.random.fold_in(rng, 1), (couples,), 0, 1 << 20) % (margin + 1)
    lengths = lengths.at[1:1 + 2 * couples:2].set(source_of - passed).at[2:2 + 2 * couples:2].set(taker + passed)
    return lengths[jax.random.permutation(jax.random.fold_in(rng, 2), number_of)]


def bell_draw(rng, dims, scale, most, shards=(), kind=jnp.bfloat16):
    level = block_scale(rng, dims, shards, -0.22, 0.18) if shards else 1.0
    result = jax.random.normal(rng, dims, jnp.float32) * scale * level
    return jnp.minimum(jnp.maximum(result, -most), most).astype(kind)


def setup_inputs(seed: int = 0, part: int = 0) -> dict:
    key_list = jax.random.split(jax.random.key(seed), 10)
    part_splits = jax.random.split(jax.random.fold_in(key_list[9], part), 10)
    hidden = draw_hidden(jax.random.fold_in(jax.random.fold_in(key_list[9], part), 71), part)
    norm_gain = jnp.clip(1.0 + 0.1 * jax.random.normal(key_list[1], (D,), jnp.float32), 0.5, 1.5).astype(jnp.bfloat16)
    head_weight = draw_head_weight(jax.random.fold_in(key_list[9], 71), part)
    gate_up = bell_draw(part_splits[3], (2, FF, TOKENS), 1.0, 6.0, ((1, 128),))
    targets = place_ends(jax.random.randint(part_splits[4], (TOKENS,), 0, VOCAB), jax.random.fold_in(part_splits[4], 1), 0, VOCAB - 1).astype(jnp.int32)
    doc_ids = jnp.searchsorted(jnp.cumsum(uneven(part_splits[5], DOCS, TOKENS, TOKENS // 4, 1)), jnp.arange(TOKENS), side="right").astype(jnp.int32)
    vocab_codes = place_ends(jax.random.randint(key_list[6], (VOCAB,), 0, 2 * RANK), jax.random.fold_in(key_list[6], 1), 0, (2 * RANK) - 1).astype(jnp.int32)
    hidden_codes = place_ends(jax.random.randint(key_list[7], (FF,), 0, 2 * RANK), jax.random.fold_in(key_list[7], 1), 0, (2 * RANK) - 1).astype(jnp.int32)
    model_codes = place_ends(jax.random.randint(key_list[8], (2, D), 0, 2 * RANK), jax.random.fold_in(key_list[8], 1), 0, (2 * RANK) - 1).astype(jnp.int32)
    return dict(hidden=hidden, norm_gain=norm_gain, head_weight=head_weight, gate_up=gate_up, targets=targets, doc_ids=doc_ids, vocab_codes=vocab_codes, hidden_codes=hidden_codes, model_codes=model_codes)


def sign_table(codes):
    slot_ids = jnp.arange(2 * RANK, dtype=jnp.int32)
    matches = (codes[:, None] == slot_ids[None, :]).astype(jnp.float32)
    return matches[:, :RANK] - matches[:, RANK:]

def doc_features(membership, left_side, right_side):
    spread = membership[:, :, None] * left_side[None, :, :]
    product = jnp.einsum('cti,tj->cij', spread, right_side, precision=lax.Precision.HIGHEST)
    return product.reshape(DOCS, RANK * RANK)

def reference(hidden, norm_gain, head_weight, gate_up, targets, doc_ids, vocab_codes, hidden_codes, model_codes):
    gain_f32 = norm_gain.astype(jnp.float32)
    values = hidden.astype(jnp.float32)
    inv_rms = lax.rsqrt(lax.optimization_barrier(jnp.mean(values * values, axis=1, keepdims=True)) + 1e-05)
    unit_rows = values * inv_rms
    normed = (unit_rows * gain_f32).astype(jnp.bfloat16)
    logits = jnp.dot(normed, head_weight.T, preferred_element_type=jnp.float32)
    row_top = lax.optimization_barrier(jnp.max(logits, axis=1, keepdims=True))
    shifted = jnp.exp(logits - row_top)
    denominator = lax.optimization_barrier(jnp.sum(shifted, axis=1, keepdims=True))
    vocab_index = jnp.arange(VOCAB, dtype=jnp.int32)
    onehot = (targets[:, None] == vocab_index[None, :]).astype(jnp.float32)
    dlogits = (shifted / denominator - onehot).astype(jnp.bfloat16)
    dnormed = jnp.dot(dlogits, head_weight, preferred_element_type=jnp.float32)
    weighted = gain_f32 * dnormed
    inner_mean = lax.optimization_barrier(jnp.mean(weighted * unit_rows, axis=1, keepdims=True))
    grad = inv_rms * (weighted - unit_rows * inner_mean)
    resid_grad = grad.astype(jnp.bfloat16)
    activation = (jax.nn.silu(gate_up[0].astype(jnp.float32)) * gate_up[1].astype(jnp.float32)).astype(jnp.bfloat16)
    vocab_sketch = jnp.dot(dlogits, sign_table(vocab_codes).astype(jnp.bfloat16), preferred_element_type=jnp.float32)
    norm_sketch = jnp.dot(normed, sign_table(model_codes[0]).astype(jnp.bfloat16), preferred_element_type=jnp.float32) * (RANK / D) ** 0.5
    act_sketch = jnp.dot(activation.T, sign_table(hidden_codes).astype(jnp.bfloat16), preferred_element_type=jnp.float32) * (RANK / FF) ** 0.5
    grad_sketch = jnp.dot(grad, sign_table(model_codes[1]), precision=lax.Precision.HIGHEST) * (RANK / D) ** 0.5
    membership = (doc_ids[None, :] == jnp.arange(DOCS, dtype=jnp.int32)[:, None]).astype(jnp.float32)
    head_features = doc_features(membership, vocab_sketch, norm_sketch)
    down_features = doc_features(membership, grad_sketch, act_sketch)
    return (resid_grad, head_features, down_features)
```

```python
import jax
import jax.numpy as jnp
from jax import lax
from jax.experimental import pallas as pl
from jax.experimental.pallas import tpu as pltpu
from jax.sharding import PartitionSpec as P

D = 4096
RANK = 64
DOCS = 8
PEERS = 64
TOK = 128
LANES = 128
PIECES = D // LANES
VOC = 512
FF = 28672
MIB = 1 << 20

f32 = jnp.float32
bf16 = jnp.bfloat16

NN = (((1,), (0,)), ((), ()))
NT = (((1,), (1,)), ((), ()))
TN = (((0,), (0,)), ((), ()))


def dot(a, b, dims, precision=None):
    return lax.dot_general(a, b, dims, precision=precision, preferred_element_type=f32)


def sign_rows(codes_row):
    slots = lax.broadcasted_iota(jnp.int32, (RANK, codes_row.shape[1]), 0)
    plus = (codes_row == slots).astype(f32)
    minus = (codes_row == slots + RANK).astype(f32)
    return (plus - minus).astype(bf16)


def token_piece(ref, piece):
    first = ref[pl.ds(piece, PEERS, stride=2 * PIECES), :]
    second = ref[pl.ds(PIECES + piece, PEERS, stride=2 * PIECES), :]
    return jnp.concatenate([first, second], axis=0)


def call(kernel, outs, scratch, n_in, flops, bytes_accessed, any_inputs=(), vmem=48 * MIB):
    specs = [
        pl.BlockSpec(memory_space=pl.ANY if i in any_inputs else pltpu.VMEM) for i in range(n_in)
    ]
    return pl.pallas_call(
        kernel,
        out_shape=outs,
        in_specs=specs,
        out_specs=jax.tree.map(lambda _: pl.BlockSpec(memory_space=pltpu.VMEM), outs),
        scratch_shapes=scratch,
        compiler_params=pltpu.CompilerParams(vmem_limit_bytes=vmem),
        cost_estimate=pl.CostEstimate(
            flops=flops, bytes_accessed=bytes_accessed, transcendentals=0
        ),
    )


def act_kernel(gate_up, codes, out):
    gate = gate_up[0].astype(f32)
    act = (gate / (1.0 + jnp.exp(-gate)) * gate_up[1].astype(f32)).astype(bf16)
    out[...] = dot(sign_rows(codes[...]), act, NN)


def table_kernel(codes, out):
    for block in range(8):
        cols = pl.ds(block * 512, 512)
        out[0:RANK, cols] = sign_rows(codes[0:1, cols])
        out[RANK : 2 * RANK, cols] = sign_rows(codes[1:2, cols])


def norm_pieces(x, gain, xf, hid, normed):
    xf[...] = x[...].astype(f32)
    squares = jnp.zeros((TOK, LANES), f32)
    for k in range(PIECES):
        piece = token_piece(xf, k)
        squares = squares + piece * piece
        hid[:, k * LANES : (k + 1) * LANES] = piece.astype(bf16)
    inv = lax.rsqrt(jnp.sum(squares, axis=1, keepdims=True) * (1.0 / D) + 1e-05)
    for k in range(PIECES):
        cols = slice(k * LANES, (k + 1) * LANES)
        unit = hid[:, cols].astype(f32) * inv
        normed[:, cols] = (unit * gain[k : k + 1, :]).astype(bf16)
    return squares


def score_kernel(x, gain, w_own, w_par, act, logits, payload, xf, hid, normed, w, sems):
    copies = []
    for block in range(4):
        source = w_own if block < 2 else w_par
        copy = pltpu.make_async_copy(
            source.at[pl.ds((block % 2) * 256, 256)], w.at[pl.ds(block * 256, 256)], sems.at[block]
        )
        copy.start()
        copies.append(copy)
    norm_pieces(x, gain, xf, hid, normed)
    for block in range(4):
        copies[block].wait()
        rows = pl.ds(block * 256, 256)
        logits[rows, :] = dot(w[rows, :], normed[...], NT)
    scores = logits[...]
    top = jnp.max(scores, axis=0, keepdims=True)
    total = jnp.sum(jnp.exp(scores - top), axis=0, keepdims=True)
    payload[pl.ds(0, PEERS, stride=4), :] = jnp.broadcast_to(top, (PEERS, LANES))
    payload[pl.ds(1, PEERS, stride=4), :] = jnp.broadcast_to(total, (PEERS, LANES))
    payload[pl.ds(2, PEERS, stride=4), :] = jnp.broadcast_to(act[...], (PEERS, LANES))
    payload[pl.ds(3, PEERS, stride=4), :] = jnp.zeros((PEERS, LANES), f32)


def norm_sketch_kernel(x, gain, table, aux, xf, hid, normed):
    squares = norm_pieces(x, gain, xf, hid, normed)
    sums = jnp.sum(squares.T, axis=0, keepdims=True)
    inv = lax.rsqrt(sums * (1.0 / D) + 1e-05)
    aux[0:RANK, :] = dot(table[0:RANK, :], normed[...], NT) * (RANK / D) ** 0.5
    aux[RANK : 2 * RANK, :] = dot(table[RANK : 2 * RANK, :], hid[...], NT) * inv
    aux[2 * RANK : 2 * RANK + 8, :] = jnp.broadcast_to(inv, (8, LANES))


def grad_kernel(stats, logits, hit, w_own, w_par, blocks, dl_out, mean_out, dn_out, df, w, sems):
    copies = []
    for chunk in range(8):
        cols = pl.ds(chunk * 512, 512)
        for half, source in enumerate((w_own, w_par)):
            copy = pltpu.make_async_copy(
                source.at[:, cols], w.at[pl.ds(half * VOC, VOC), cols], sems.at[chunk, half]
            )
            copy.start()
            copies.append(copy)
    tops = stats[pl.ds(0, PEERS, stride=4), :]
    totals = stats[pl.ds(1, PEERS, stride=4), :]
    top = jnp.max(tops, axis=0, keepdims=True)
    denominator = jnp.sum(totals * jnp.exp(tops - top), axis=0, keepdims=True)
    scores = logits[...]
    rows = lax.broadcasted_iota(jnp.int32, (2 * VOC, LANES), 0)
    onehot = (rows == hit[0:1, :]).astype(f32)
    dl32 = jnp.exp(scores - top) / denominator - onehot
    dl = dl32.astype(bf16)
    dl_out[...] = dl
    mean = jnp.sum(dl.astype(f32) * scores, axis=0, keepdims=True) * (1.0 / D)
    mean_out[...] = jnp.broadcast_to(mean, (8, LANES))
    dl_t = dl32.T.astype(bf16)
    for chunk in range(8):
        copies[2 * chunk].wait()
        copies[2 * chunk + 1].wait()
        cols = slice(chunk * 512, (chunk + 1) * 512)
        dn = dot(dl_t, w[:, cols], NN)
        dn_out[:, cols] = dn
        for k in range(4):
            piece = chunk * 4 + k
            lanes = slice(k * LANES, (k + 1) * LANES)
            df[pl.ds(piece, PEERS, stride=2 * PIECES), :] = dn[0:PEERS, lanes]
            df[pl.ds(PIECES + piece, PEERS, stride=2 * PIECES), :] = dn[PEERS:TOK, lanes]
    blocks[...] = df[...].astype(bf16)


def sketch_kernel(dl, mean, dn, codes, table, gain, aux, columns):
    vocab_sketch = dot(sign_rows(codes[...]), dl[...], NN)
    weighted = dn[...] * gain[...]
    high = weighted.astype(bf16)
    low = (weighted - high.astype(f32)).astype(bf16)
    signs = table[RANK : 2 * RANK, :]
    sketch = dot(signs, high, NT) + dot(signs, low, NT)
    unit_sketch = aux[RANK : 2 * RANK, :]
    inv = aux[2 * RANK : 2 * RANK + 1, :]
    grad_sketch = inv * (sketch - unit_sketch * mean[0:1, :]) * (RANK / D) ** 0.5
    columns[pl.ds(0, PEERS, stride=2), :] = vocab_sketch
    columns[pl.ds(1, PEERS, stride=2), :] = grad_sketch


def feature_kernel(columns, stats, aux, docs, out):
    vocab_column = jnp.sum(columns[pl.ds(0, PEERS, stride=2), :], axis=0, keepdims=True)
    grad_column = jnp.sum(columns[pl.ds(1, PEERS, stride=2), :], axis=0, keepdims=True)
    acts = stats[pl.ds(2, PEERS, stride=4), :]
    act_sketch = jnp.concatenate([acts[:, 0:RANK], acts[:, RANK : 2 * RANK]], axis=0)
    act_sketch = act_sketch * (RANK / FF) ** 0.5
    ids = lax.broadcasted_iota(jnp.int32, (DOCS, LANES), 0)
    member = (docs[0:1, :] == ids).astype(f32)
    high = lax.Precision.HIGHEST
    out[0:DOCS, :] = dot(member * vocab_column, aux[0:RANK, :], NT, high)
    out[DOCS : 2 * DOCS, :] = dot(member * grad_column, act_sketch, NN, high)


def resid_kernel(blocks, hidden, gain, out):
    total = jnp.zeros((2 * PIECES, LANES), f32)
    for source in range(PEERS):
        total = total + blocks[source * 2 * PIECES : (source + 1) * 2 * PIECES, :].astype(f32)
    for token in range(2):
        rows = slice(token * PIECES, (token + 1) * PIECES)
        values = hidden[rows, :].astype(f32)
        inv = lax.rsqrt(jnp.sum(values * values, keepdims=True) * (1.0 / D) + 1e-05)
        unit = values * inv
        weighted = gain[...] * total[rows, :]
        inner = jnp.sum(weighted * unit, keepdims=True) * (1.0 / D)
        out[rows, :] = (inv * (weighted - unit * inner)).astype(bf16)


def shards(
    hidden,
    norm_gain,
    head_weight,
    gate_up,
    targets,
    doc_ids,
    vocab_codes,
    hidden_codes,
    model_codes,
):
    index = lax.axis_index("tensor")
    core = lax.rem(index, 2)
    groups = [list(range(0, 2 * PEERS, 2)), list(range(1, 2 * PEERS, 2))]
    partner = [(i, i ^ 1) for i in range(2 * PEERS)]
    gain32 = norm_gain.astype(f32)
    gain_row = gain32.reshape(1, D)
    gain_blk = gain32.reshape(PIECES, LANES)
    own_rows = hidden.reshape(2 * PIECES, LANES)

    def exchange(rows):
        return lax.all_to_all(rows, "tensor", 0, 0, axis_index_groups=groups, tiled=True)

    with jax.named_scope("gather_hidden"):
        spread = jnp.broadcast_to(own_rows[None], (PEERS, 2 * PIECES, LANES))
        gathered = exchange(spread).reshape(PEERS * 2 * PIECES, LANES)
    with jax.named_scope("partner_rows"):
        w_par = lax.ppermute(head_weight, "tensor", partner)
        codes_par = lax.ppermute(vocab_codes, "tensor", partner)
        codes = jnp.concatenate([vocab_codes, codes_par]).reshape(1, 2 * VOC)
    with jax.named_scope("activations"):
        act_part = call(act_kernel, jax.ShapeDtypeStruct((RANK, 256), f32), [], 2, 8000000, 300000)(
            gate_up, hidden_codes.reshape(1, -1)
        )
        act_blocks = act_part.T.reshape(2 * PEERS, 1, LANES)
        act_all = lax.all_to_all(act_blocks, "tensor", 0, 0, tiled=True)
        act_own = jnp.sum(act_all, axis=0)
    with jax.named_scope("tables"):
        table = call(
            table_kernel, jax.ShapeDtypeStruct((2 * RANK, D), bf16), [], 1, 4000000, 1100000
        )(model_codes)
        ids = jnp.stack([targets, doc_ids]).reshape(2, PEERS, 2, 2)
        ids = lax.dynamic_index_in_dim(ids, core, axis=2, keepdims=False)
        ids = ids.transpose(0, 2, 1).reshape(2, TOK)
        relative = ids[0] - index * VOC
        relative_par = ids[0] - (index + 1 - 2 * core) * VOC
        hit = jnp.where(
            (relative >= 0) & (relative < VOC),
            relative,
            jnp.where((relative_par >= 0) & (relative_par < VOC), relative_par + VOC, -1),
        ).reshape(1, TOK)
        docs = ids[1].reshape(1, TOK)

    norm_scratch = [
        pltpu.VMEM((PEERS * 2 * PIECES, LANES), f32),
        pltpu.VMEM((TOK, D), bf16),
        pltpu.VMEM((TOK, D), bf16),
    ]
    with jax.named_scope("scores"):
        logits, payload = call(
            score_kernel,
            (
                jax.ShapeDtypeStruct((2 * VOC, TOK), f32),
                jax.ShapeDtypeStruct((PEERS * 4, LANES), f32),
            ),
            norm_scratch + [pltpu.VMEM((2 * VOC, D), bf16), pltpu.SemaphoreType.DMA((4,))],
            5,
            1 << 30,
            10 * MIB,
            any_inputs=(2, 3),
        )(gathered, gain_blk, head_weight, w_par, act_own)
    with jax.named_scope("statistics"):
        stats = exchange(payload.reshape(PEERS, 4, LANES)).reshape(PEERS * 4, LANES)
    with jax.named_scope("norm_sketch"):
        aux = call(
            norm_sketch_kernel,
            jax.ShapeDtypeStruct((2 * RANK + 8, LANES), f32),
            norm_scratch,
            3,
            200000000,
            3 * MIB,
        )(gathered, gain_blk, table)
    with jax.named_scope("dnormed"):
        blocks, dl, mean, dn = call(
            grad_kernel,
            (
                jax.ShapeDtypeStruct((PEERS * 2 * PIECES, LANES), bf16),
                jax.ShapeDtypeStruct((2 * VOC, TOK), bf16),
                jax.ShapeDtypeStruct((8, LANES), f32),
                jax.ShapeDtypeStruct((TOK, D), f32),
            ),
            [
                pltpu.VMEM((PEERS * 2 * PIECES, LANES), f32),
                pltpu.VMEM((2 * VOC, D), bf16),
                pltpu.SemaphoreType.DMA((8, 2)),
            ],
            5,
            1 << 30,
            12 * MIB,
            any_inputs=(3, 4),
        )(stats, logits, hit, head_weight, w_par)
    with jax.named_scope("scatter_dnormed"):
        received = exchange(blocks.reshape(PEERS, 2 * PIECES, LANES))
        received = received.reshape(PEERS * 2 * PIECES, LANES)
    with jax.named_scope("sketches"):
        columns = call(
            sketch_kernel,
            jax.ShapeDtypeStruct((2 * PEERS, LANES), f32),
            [],
            7,
            200000000,
            4 * MIB,
        )(dl, mean, dn, codes, table, gain_row, aux)
        columns = exchange(columns.reshape(PEERS, 2, LANES)).reshape(2 * PEERS, LANES)
    with jax.named_scope("features"):
        features = call(
            feature_kernel,
            jax.ShapeDtypeStruct((2 * DOCS, RANK), f32),
            [],
            4,
            2000000,
            300000,
        )(columns, stats, aux, docs)
        half = RANK // 2
        mine = lax.dynamic_slice_in_dim(features, core * half, half, 1)
        other = lax.dynamic_slice_in_dim(features, (1 - core) * half, half, 1)
        features = mine + lax.ppermute(other, "tensor", partner)
    with jax.named_scope("resid_grad"):
        resid = call(
            resid_kernel,
            jax.ShapeDtypeStruct((2 * PIECES, LANES), bf16),
            [],
            3,
            2000000,
            MIB,
        )(received, own_rows, gain_blk)
        resid = resid.reshape(2, D)
    return resid, features[:DOCS], features[DOCS:]


def solution(mesh):
    in_specs = (
        P(("dp", "tensor"), None),
        P(),
        P("tensor", None),
        P(None, "tensor", "dp"),
        P("dp"),
        P("dp"),
        P("tensor"),
        P("tensor"),
        P(),
    )
    out_specs = (P(("dp", "tensor"), None), P("dp", "tensor"), P("dp", "tensor"))
    return jax.shard_map(shards, mesh=mesh, in_specs=in_specs, out_specs=out_specs, check_vma=False)
```

```python
import jax
import jax.numpy as jnp
from jax import lax
from jax.experimental import pallas as pl
from jax.experimental.pallas import tpu as pltpu
from jax.sharding import PartitionSpec as P

D = 4096
RANK = 64
DOCS = 8
PEERS = 64
TOK = 128
LANES = 128
PIECES = D // LANES
VOC = 512
FF = 28672
PITCH = 2 * PIECES + 8
CHUNK = 512
MIB = 1 << 20

f32 = jnp.float32
bf16 = jnp.bfloat16

NN = (((1,), (0,)), ((), ()))
NT = (((1,), (1,)), ((), ()))
TN = (((0,), (0,)), ((), ()))


def dot(a, b, dims, precision=None):
    return lax.dot_general(a, b, dims, precision=precision, preferred_element_type=f32)


def sign_rows(codes_row):
    slots = lax.broadcasted_iota(jnp.int32, (RANK, codes_row.shape[1]), 0)
    plus = (codes_row == slots).astype(f32)
    minus = (codes_row == slots + RANK).astype(f32)
    return (plus - minus).astype(bf16)


def token_piece(ref, piece):
    first = ref[pl.ds(piece, PEERS, stride=PITCH), :]
    second = ref[pl.ds(PIECES + piece, PEERS, stride=PITCH), :]
    return jnp.concatenate([first, second], axis=0)


def call(kernel, outs, scratch, n_in, flops, bytes_accessed, any_inputs=(), any_outs=(), vmem=32 * MIB):
    specs = [
        pl.BlockSpec(memory_space=pltpu.HBM if i in any_inputs else pltpu.VMEM) for i in range(n_in)
    ]
    leaves, tree = jax.tree.flatten(outs)
    out_specs = tree.unflatten(
        [
            pl.BlockSpec(memory_space=pltpu.HBM if i in any_outs else pltpu.VMEM)
            for i in range(len(leaves))
        ]
    )
    leaves = [
        pltpu.HBM(leaf.shape, leaf.dtype) if i in any_outs else leaf
        for i, leaf in enumerate(leaves)
    ]
    inner = pl.pallas_call(
        kernel,
        out_shape=tree.unflatten(leaves),
        in_specs=specs,
        out_specs=out_specs,
        scratch_shapes=scratch,
        compiler_params=pltpu.CompilerParams(vmem_limit_bytes=vmem),
        cost_estimate=pl.CostEstimate(
            flops=flops, bytes_accessed=bytes_accessed, transcendentals=0
        ),
    )

    def run(*args):
        return inner(
            *[
                pltpu.with_memory_space_constraint(arg, pltpu.HBM) if i in any_inputs else arg
                for i, arg in enumerate(args)
            ]
        )

    return run


def spread_kernel(rows, out):
    pieces = [rows[:, k * LANES : (k + 1) * LANES].astype(f32) for k in range(PIECES)]
    stacked = jnp.concatenate([p[0:1, :] for p in pieces] + [p[1:2, :] for p in pieces], axis=0)
    stacked = stacked.astype(bf16)
    for peer in range(PEERS):
        out[peer, :, :] = stacked


def act_kernel(gate_up, codes, out):
    gate = gate_up[0].astype(f32)
    act = (gate / (1.0 + jnp.exp(-gate)) * gate_up[1].astype(f32)).astype(bf16)
    out[...] = dot(sign_rows(codes[...]), act, NN)


def table_kernel(codes, out):
    for block in range(8):
        cols = pl.ds(block * 512, 512)
        out[0:RANK, cols] = sign_rows(codes[0:1, cols])
        out[RANK : 2 * RANK, cols] = sign_rows(codes[1:2, cols])


def norm_pieces(x, gain, xf, hid, normed):
    for peer in range(PEERS):
        rows = slice(peer * 2 * PIECES, (peer + 1) * 2 * PIECES)
        xf[peer * PITCH : peer * PITCH + 2 * PIECES, :] = x[rows, :].astype(f32)
    squares = jnp.zeros((TOK, LANES), f32)
    for k in range(PIECES):
        piece = token_piece(xf, k)
        squares = squares + piece * piece
        hid[:, k * LANES : (k + 1) * LANES] = piece.astype(bf16)
    inv = lax.rsqrt(jnp.sum(squares, axis=1, keepdims=True) * (1.0 / D) + 1e-05)
    for k in range(PIECES):
        cols = slice(k * LANES, (k + 1) * LANES)
        unit = hid[:, cols].astype(f32) * inv
        normed[:, cols] = (unit * gain[k : k + 1, :]).astype(bf16)
    return squares


def score_kernel(x, gain, w_own, w_par, acts, logits, payload, xf, hid, normed, w, sems):
    copies = []
    for block in range(4):
        source = w_own if block < 2 else w_par
        copy = pltpu.make_async_copy(
            source.at[pl.ds((block % 2) * 256, 256)], w.at[pl.ds(block * 256, 256)], sems.at[block]
        )
        copy.start()
        copies.append(copy)
    norm_pieces(x, gain, xf, hid, normed)
    for block in range(4):
        copies[block].wait()
        part = slice(block * 256, (block + 1) * 256)
        logits[part, :] = dot(w[part, :], normed[...], NT)
    scores = logits[...]
    top = jnp.max(scores, axis=0, keepdims=True)
    total = jnp.sum(jnp.exp(scores - top), axis=0, keepdims=True)
    payload[pl.ds(0, PEERS, stride=4), :] = jnp.broadcast_to(top, (PEERS, LANES))
    payload[pl.ds(1, PEERS, stride=4), :] = jnp.broadcast_to(total, (PEERS, LANES))
    payload[pl.ds(2, PEERS, stride=4), :] = acts[...]
    payload[pl.ds(3, PEERS, stride=4), :] = jnp.zeros((PEERS, LANES), f32)


def split(values):
    high = values.astype(bf16)
    return high, (values - high.astype(f32)).astype(bf16)


def backward_kernel(
    logits, hit, codes, table, gain_row, x, gain, w_own, w_par,
    soft_out, picked_out, columns, aux,
    xf, hid, normed, w, soft, picked, w_sems, out_sems,
):
    chunks = D // CHUNK
    copies = []
    for chunk in range(chunks):
        cols = pl.ds(chunk * CHUNK, CHUNK)
        for half, source in enumerate((w_own, w_par)):
            copy = pltpu.make_async_copy(
                source.at[:, cols], w.at[pl.ds(half * VOC, VOC), cols], w_sems.at[chunk, half]
            )
            copy.start()
            copies.append(copy)
    squares = norm_pieces(x, gain, xf, hid, normed)
    sums = jnp.sum(squares.T, axis=0, keepdims=True)
    inv = lax.rsqrt(sums * (1.0 / D) + 1e-05)
    unit_sketch = dot(table[RANK : 2 * RANK, :], hid[...], NT) * inv
    inv = inv * (RANK / D) ** 0.5
    aux[...] = dot(table[0:RANK, :], normed[...], NT) * (RANK / D) ** 0.5
    scores = logits[...]
    top = jnp.max(scores, axis=0, keepdims=True)
    rows = lax.broadcasted_iota(jnp.int32, (2 * VOC, LANES), 0)
    chosen = rows == hit[0:1, :]
    onehot = chosen.astype(f32)
    weights = jnp.exp(scores - top)
    others = jnp.where(chosen, 0.0, weights)
    at_target = jnp.sum(jnp.where(chosen, weights, 0.0), axis=0, keepdims=True)
    at_target_rows = jnp.broadcast_to(at_target, (LANES, LANES)).T
    high, low = split(others)
    left = jnp.concatenate(
        [others.T.astype(bf16), low.astype(f32).T.astype(bf16), onehot.T.astype(bf16)], axis=0
    )
    sums = jnp.zeros((RANK, 4 * TOK), f32)
    outs = []
    for chunk in range(chunks):
        copies[2 * chunk].wait()
        copies[2 * chunk + 1].wait()
        cols = slice(chunk * CHUNK, (chunk + 1) * CHUNK)
        both = dot(left, w[:, cols], NN)
        pick = both[2 * TOK :, :]
        full = both[0:TOK, :] + both[TOK : 2 * TOK, :]
        for k in range(CHUNK // LANES):
            lanes = slice(k * LANES, (k + 1) * LANES)
            place = slice(chunk * CHUNK + k * LANES, chunk * CHUNK + (k + 1) * LANES)
            soft[:, place] = full[:, lanes] + at_target_rows * pick[:, lanes]
        picked[:, cols] = pick.astype(bf16)
        spot = pl.ds(chunk * CHUNK, CHUNK)
        for sem, (source, target) in enumerate(((soft, soft_out), (picked, picked_out))):
            copy = pltpu.make_async_copy(
                source.at[:, spot], target.at[:, spot], out_sems.at[chunk, sem]
            )
            copy.start()
            outs.append(copy)
        full_high, full_low = split(soft[:, cols] * gain_row[:, cols])
        pick_high, pick_low = split(pick * gain_row[:, cols])
        right = jnp.concatenate([full_high, full_low, pick_high, pick_low], axis=0)
        sums = sums + dot(table[RANK : 2 * RANK, cols], right, NT)
    full_sketch = sums[:, 0:TOK] + sums[:, TOK : 2 * TOK]
    pick_sketch = sums[:, 2 * TOK : 3 * TOK] + sums[:, 3 * TOK :]
    full_mean = jnp.sum(weights * scores, axis=0, keepdims=True) * (1.0 / D)
    pick_mean = jnp.sum(onehot * scores, axis=0, keepdims=True) * (1.0 / D)
    signs = sign_rows(codes[...])
    pick_vocab = dot(signs, onehot.astype(bf16), NN)
    soft_vocab = dot(signs, high, NN) + dot(signs, low, NN) + at_target * pick_vocab
    columns[0:RANK, :] = soft_vocab
    columns[RANK : 2 * RANK, :] = pick_vocab
    columns[2 * RANK : 3 * RANK, :] = inv * (full_sketch - unit_sketch * full_mean)
    columns[3 * RANK : 4 * RANK, :] = inv * (pick_sketch - unit_sketch * pick_mean)
    columns[4 * RANK : 4 * RANK + 8, :] = jnp.broadcast_to(top, (8, LANES))
    for copy in outs:
        copy.wait()


def scale_kernel(stats, soft_in, picked_in, columns, blocks, df, soft, picked, sems):
    copies = []
    for chunk in range(D // CHUNK):
        cols = pl.ds(chunk * CHUNK, CHUNK)
        for sem, (source, target) in enumerate(((soft_in, soft), (picked_in, picked))):
            copy = pltpu.make_async_copy(
                source.at[:, cols], target.at[:, cols], sems.at[chunk, sem]
            )
            copy.start()
            copies.append(copy)
    tops = stats[pl.ds(0, PEERS, stride=4), :]
    totals = stats[pl.ds(1, PEERS, stride=4), :]
    acts = jnp.sum(stats[pl.ds(2, PEERS, stride=4), :], axis=0, keepdims=True)
    top = jnp.max(tops, axis=0, keepdims=True)
    denominator = jnp.sum(totals * jnp.exp(tops - top), axis=0, keepdims=True)
    scale = jnp.exp(columns[4 * RANK : 4 * RANK + 1, :] - top) / denominator
    scale_rows = jnp.broadcast_to(scale, (LANES, LANES)).T
    for k in range(PIECES):
        if k % (CHUNK // LANES) == 0:
            chunk = k // (CHUNK // LANES)
            copies[2 * chunk].wait()
            copies[2 * chunk + 1].wait()
        lanes = slice(k * LANES, (k + 1) * LANES)
        piece = scale_rows * soft[:, lanes] - picked[:, lanes].astype(f32)
        df[pl.ds(k, PEERS, stride=PITCH), :] = piece[0:PEERS, :]
        df[pl.ds(PIECES + k, PEERS, stride=PITCH), :] = piece[PEERS:TOK, :]
    vocab_sketch = scale * columns[0:RANK, :] - columns[RANK : 2 * RANK, :]
    grad_sketch = scale * columns[2 * RANK : 3 * RANK, :] - columns[3 * RANK : 4 * RANK, :]
    acts = jnp.broadcast_to(acts, (PEERS, LANES))
    for place, values in enumerate((vocab_sketch, grad_sketch, acts)):
        high = values.astype(bf16).astype(f32)
        df[pl.ds(2 * PIECES + 2 * place, PEERS, stride=PITCH), :] = high
        df[pl.ds(2 * PIECES + 2 * place + 1, PEERS, stride=PITCH), :] = values - high
    for row in (6, 7):
        df[pl.ds(2 * PIECES + row, PEERS, stride=PITCH), :] = jnp.zeros((PEERS, LANES), f32)
    blocks[...] = df[...].reshape(PEERS, PITCH, LANES).astype(bf16)


def feature_kernel(blocks, aux, docs, core, mine, other, rows):
    rows[...] = blocks[...].astype(f32)[:, 2 * PIECES :, :].reshape(PEERS * 8, LANES)

    def row(place):
        return rows[pl.ds(place, PEERS, stride=8), :]

    vocab_column = jnp.sum(row(0) + row(1), axis=0, keepdims=True)
    grad_column = jnp.sum(row(2) + row(3), axis=0, keepdims=True)
    acts = row(4) + row(5)
    act_sketch = jnp.concatenate([acts[:, 0:RANK], acts[:, RANK : 2 * RANK]], axis=0)
    act_sketch = act_sketch * (RANK / FF) ** 0.5
    ids = lax.broadcasted_iota(jnp.int32, (DOCS, LANES), 0)
    member = (docs[0:1, :] == ids).astype(f32)
    high = lax.Precision.HIGHEST
    head = dot(member * vocab_column, aux[...], NT, high)
    down = dot(member * grad_column, act_sketch, NN, high)
    both = jnp.concatenate([head, down], axis=0)
    first, second = both[:, 0 : RANK // 2], both[:, RANK // 2 :]
    is_first = core[0:1, 0:1] == 0
    mine[...] = jnp.where(is_first, first, second)
    other[...] = jnp.where(is_first, second, first)


def resid_kernel(blocks, hidden, gain, out):
    received = blocks[...].astype(f32)
    total = jnp.zeros((2 * PIECES, LANES), f32)
    for source in range(PEERS):
        total = total + received[source, 0 : 2 * PIECES, :]
    grads = []
    for token in range(2):
        rows = slice(token * PIECES, (token + 1) * PIECES)
        values = hidden[rows, :].astype(f32)
        inv = lax.rsqrt(jnp.sum(values * values, keepdims=True) * (1.0 / D) + 1e-05)
        unit = values * inv
        weighted = gain[...] * total[rows, :]
        inner = jnp.sum(weighted * unit, keepdims=True) * (1.0 / D)
        grads.append(inv * (weighted - unit * inner))
    for k in range(PIECES):
        pair = jnp.concatenate([grads[0][k : k + 1, :], grads[1][k : k + 1, :]], axis=0)
        out[:, k * LANES : (k + 1) * LANES] = pair.astype(bf16)


def shards(
    hidden,
    norm_gain,
    head_weight,
    gate_up,
    targets,
    doc_ids,
    vocab_codes,
    hidden_codes,
    model_codes,
):
    index = lax.axis_index("tensor")
    core = lax.rem(index, 2)
    groups = [list(range(0, 2 * PEERS, 2)), list(range(1, 2 * PEERS, 2))]
    partner = [(i, i ^ 1) for i in range(2 * PEERS)]
    gain32 = norm_gain.astype(f32)
    gain_row = gain32.reshape(1, D)
    gain_blk = gain32.reshape(PIECES, LANES)
    own_rows = hidden.reshape(2 * PIECES, LANES)

    def exchange(rows):
        return lax.all_to_all(rows, "tensor", 0, 0, axis_index_groups=groups, tiled=True)

    with jax.named_scope("gather_hidden"):
        spread = call(
            spread_kernel,
            jax.ShapeDtypeStruct((PEERS, 2 * PIECES, LANES), bf16),
            [],
            1,
            1000,
            MIB,
        )(hidden)
        gathered = exchange(spread).reshape(PEERS * 2 * PIECES, LANES)
    with jax.named_scope("partner_rows"):
        w_par = lax.ppermute(head_weight, "tensor", partner)
    with jax.named_scope("activations"):
        act_part = call(act_kernel, jax.ShapeDtypeStruct((RANK, 256), f32), [], 2, 8000000, 300000)(
            gate_up, hidden_codes.reshape(1, -1)
        )
        act_part = act_part.T.reshape(PEERS, 2, LANES)
        act_mine = lax.dynamic_index_in_dim(act_part, core, axis=1, keepdims=False)
        act_other = lax.dynamic_index_in_dim(act_part, 1 - core, axis=1, keepdims=False)
        codes_own = vocab_codes.astype(f32).reshape(VOC // LANES, LANES)
        sent = jnp.concatenate([act_other, codes_own], axis=0)
        came = lax.ppermute(sent, "tensor", partner)
        acts = act_mine + came[:PEERS]
        codes_par = came[PEERS:].astype(jnp.int32).reshape(1, VOC)
        codes = jnp.concatenate([vocab_codes.reshape(1, VOC), codes_par], axis=1)
    with jax.named_scope("tables"):
        table = call(
            table_kernel, jax.ShapeDtypeStruct((2 * RANK, D), bf16), [], 1, 4000000, 1100000
        )(model_codes)
        ids = jnp.stack([targets, doc_ids]).reshape(2, PEERS, 2, 2)
        ids = lax.dynamic_index_in_dim(ids, core, axis=2, keepdims=False)
        ids = ids.transpose(0, 2, 1).reshape(2, TOK)
        relative = ids[0] - index * VOC
        relative_par = ids[0] - (index + 1 - 2 * core) * VOC
        hit = jnp.where(
            (relative >= 0) & (relative < VOC),
            relative,
            jnp.where((relative_par >= 0) & (relative_par < VOC), relative_par + VOC, -1),
        ).reshape(1, TOK)
        docs = ids[1].reshape(1, TOK)
        core_row = jnp.full((1, LANES), core, jnp.int32)

    norm_scratch = [
        pltpu.VMEM((PEERS * PITCH, LANES), f32),
        pltpu.VMEM((TOK, D), bf16),
        pltpu.VMEM((TOK, D), bf16),
    ]
    with jax.named_scope("scores"):
        logits, payload = call(
            score_kernel,
            (
                jax.ShapeDtypeStruct((2 * VOC, TOK), f32),
                jax.ShapeDtypeStruct((PEERS * 4, LANES), f32),
            ),
            norm_scratch + [pltpu.VMEM((2 * VOC, D), bf16), pltpu.SemaphoreType.DMA((4,))],
            5,
            1 << 30,
            10 * MIB,
            any_inputs=(2, 3),
        )(gathered, gain_blk, head_weight, w_par, acts)
    with jax.named_scope("statistics"):
        stats = exchange(payload.reshape(PEERS, 4, LANES)).reshape(PEERS * 4, LANES)
    with jax.named_scope("backward"):
        soft, picked, columns, aux = call(
            backward_kernel,
            (
                jax.ShapeDtypeStruct((TOK, D), f32),
                jax.ShapeDtypeStruct((TOK, D), bf16),
                jax.ShapeDtypeStruct((4 * RANK + 8, LANES), f32),
                jax.ShapeDtypeStruct((RANK, LANES), f32),
            ),
            norm_scratch
            + [
                pltpu.VMEM((2 * VOC, D), bf16),
                pltpu.VMEM((TOK, D), f32),
                pltpu.VMEM((TOK, D), bf16),
                pltpu.SemaphoreType.DMA((D // CHUNK, 2)),
                pltpu.SemaphoreType.DMA((D // CHUNK, 2)),
            ],
            9,
            3 << 30,
            12 * MIB,
            any_inputs=(7, 8),
            any_outs=(0, 1),
        )(logits, hit, codes, table, gain_row, gathered, gain_blk, head_weight, w_par)
    with jax.named_scope("scale"):
        blocks = call(
            scale_kernel,
            jax.ShapeDtypeStruct((PEERS, PITCH, LANES), bf16),
            [
                pltpu.VMEM((PEERS * PITCH, LANES), f32),
                pltpu.VMEM((TOK, D), f32),
                pltpu.VMEM((TOK, D), bf16),
                pltpu.SemaphoreType.DMA((D // CHUNK, 2)),
            ],
            4,
            2000000,
            4 * MIB,
            any_inputs=(1, 2),
        )(stats, soft, picked, columns)
    with jax.named_scope("scatter_dnormed"):
        blocks, docs, core_row, gain_blk, aux, own_rows = lax.optimization_barrier(
            (blocks, docs, core_row, gain_blk, aux, own_rows)
        )
        received = exchange(blocks)
    with jax.named_scope("features"):
        half = jax.ShapeDtypeStruct((2 * DOCS, RANK // 2), f32)
        mine, other = call(
            feature_kernel,
            (half, half),
            [pltpu.VMEM((PEERS * 8, LANES), f32)],
            4,
            2000000,
            300000,
        )(received, aux, docs, core_row)
        features = mine + lax.ppermute(other, "tensor", partner)
    with jax.named_scope("resid_grad"):
        resid = call(
            resid_kernel,
            jax.ShapeDtypeStruct((2, D), bf16),
            [],
            3,
            2000000,
            MIB,
        )(received, own_rows, gain_blk)
    return resid, features[:DOCS], features[DOCS:]


def solution(mesh):
    in_specs = (
        P(("dp", "tensor"), None),
        P(),
        P("tensor", None),
        P(None, "tensor", "dp"),
        P("dp"),
        P("dp"),
        P("tensor"),
        P("tensor"),
        P(),
    )
    out_specs = (P(("dp", "tensor"), None), P("dp", "tensor"), P("dp", "tensor"))
    return jax.shard_map(shards, mesh=mesh, in_specs=in_specs, out_specs=out_specs, check_vma=False)
```

```python
import jax
import jax.numpy as jnp
from jax import lax
from jax.experimental import pallas as pl
from jax.experimental.pallas import tpu as pltpu
from jax.sharding import PartitionSpec as P

D = 4096
RANK = 64
DOCS = 8
PEERS = 64
TOK = 128
LANES = 128
PIECES = D // LANES
VOC = 512
FF = 28672
PITCH = 2 * PIECES + 8
CHUNK = 1024
MIB = 1 << 20

f32 = jnp.float32
bf16 = jnp.bfloat16

NN = (((1,), (0,)), ((), ()))
NT = (((1,), (1,)), ((), ()))
TN = (((0,), (0,)), ((), ()))


def dot(a, b, dims, precision=None):
    return lax.dot_general(a, b, dims, precision=precision, preferred_element_type=f32)


def sign_rows(codes_row):
    slots = lax.broadcasted_iota(jnp.int32, (RANK, codes_row.shape[1]), 0)
    plus = (codes_row == slots).astype(f32)
    minus = (codes_row == slots + RANK).astype(f32)
    return (plus - minus).astype(bf16)


def token_piece(ref, piece):
    first = ref[pl.ds(piece, PEERS, stride=PITCH), :]
    second = ref[pl.ds(PIECES + piece, PEERS, stride=PITCH), :]
    return jnp.concatenate([first, second], axis=0)


def call(kernel, outs, scratch, n_in, flops, bytes_accessed, any_inputs=(), any_outs=(), vmem=32 * MIB):
    specs = [
        pl.BlockSpec(memory_space=pltpu.HBM if i in any_inputs else pltpu.VMEM) for i in range(n_in)
    ]
    leaves, tree = jax.tree.flatten(outs)
    out_specs = tree.unflatten(
        [
            pl.BlockSpec(memory_space=pltpu.HBM if i in any_outs else pltpu.VMEM)
            for i in range(len(leaves))
        ]
    )
    leaves = [
        pltpu.HBM(leaf.shape, leaf.dtype) if i in any_outs else leaf
        for i, leaf in enumerate(leaves)
    ]
    inner = pl.pallas_call(
        kernel,
        out_shape=tree.unflatten(leaves),
        in_specs=specs,
        out_specs=out_specs,
        scratch_shapes=scratch,
        compiler_params=pltpu.CompilerParams(vmem_limit_bytes=vmem),
        cost_estimate=pl.CostEstimate(
            flops=flops, bytes_accessed=bytes_accessed, transcendentals=0
        ),
    )

    def run(*args):
        return inner(
            *[
                pltpu.with_memory_space_constraint(arg, pltpu.HBM) if i in any_inputs else arg
                for i, arg in enumerate(args)
            ]
        )

    return run


def spread_kernel(rows, out):
    pieces = [rows[:, k * LANES : (k + 1) * LANES].astype(f32) for k in range(PIECES)]
    stacked = jnp.concatenate([p[0:1, :] for p in pieces] + [p[1:2, :] for p in pieces], axis=0)
    stacked = stacked.astype(bf16)
    for peer in range(PEERS):
        out[peer, :, :] = stacked


def act_kernel(gate_up, codes, out):
    gate = gate_up[0].astype(f32)
    act = (gate / (1.0 + jnp.exp(-gate)) * gate_up[1].astype(f32)).astype(bf16)
    out[...] = dot(sign_rows(codes[...]), act, NN)


def table_kernel(codes, out):
    for block in range(8):
        cols = pl.ds(block * 512, 512)
        out[0:RANK, cols] = sign_rows(codes[0:1, cols])
        out[RANK : 2 * RANK, cols] = sign_rows(codes[1:2, cols])


def norm_pieces(x, gain, xf, hid, normed):
    for peer in range(PEERS):
        rows = slice(peer * 2 * PIECES, (peer + 1) * 2 * PIECES)
        xf[peer * PITCH : peer * PITCH + 2 * PIECES, :] = x[rows, :].astype(f32)
    squares = jnp.zeros((TOK, LANES), f32)
    for k in range(PIECES):
        piece = token_piece(xf, k)
        squares = squares + piece * piece
        hid[:, k * LANES : (k + 1) * LANES] = piece.astype(bf16)
    inv = lax.rsqrt(jnp.sum(squares, axis=1, keepdims=True) * (1.0 / D) + 1e-05)
    for k in range(PIECES):
        cols = slice(k * LANES, (k + 1) * LANES)
        unit = hid[:, cols].astype(f32) * inv
        normed[:, cols] = (unit * gain[k : k + 1, :]).astype(bf16)
    return squares


def score_kernel(x, gain, w_own, w_par, acts, logits, payload, xf, hid, normed, w, sems):
    copies = [
        pltpu.make_async_copy(source, w.at[pl.ds(half * VOC, VOC)], sems.at[half])
        for half, source in enumerate((w_own, w_par))
    ]
    copies[0].start()
    norm_pieces(x, gain, xf, hid, normed)
    copies[1].start()
    for half in range(2):
        copies[half].wait()
        part = slice(half * VOC, (half + 1) * VOC)
        logits[part, :] = dot(normed[...], w[part, :], NT).T
    scores = logits[...]
    top = jnp.max(scores, axis=0, keepdims=True)
    total = jnp.sum(jnp.exp(scores - top), axis=0, keepdims=True)
    payload[pl.ds(0, PEERS, stride=4), :] = jnp.broadcast_to(top, (PEERS, LANES))
    payload[pl.ds(1, PEERS, stride=4), :] = jnp.broadcast_to(total, (PEERS, LANES))
    payload[pl.ds(2, PEERS, stride=4), :] = acts[...]
    payload[pl.ds(3, PEERS, stride=4), :] = jnp.zeros((PEERS, LANES), f32)


def split(values):
    high = values.astype(bf16)
    return high, (values - high.astype(f32)).astype(bf16)


def backward_kernel(
    logits, hit, codes, table, gain_row, x, gain, w_own, w_par,
    soft_out, picked_out, columns, aux,
    xf, hid, normed, w, soft, picked, w_sems, out_sems,
):
    chunks = D // CHUNK
    copies = []
    for chunk in range(chunks):
        cols = pl.ds(chunk * CHUNK, CHUNK)
        for half, source in enumerate((w_own, w_par)):
            copies.append(
                pltpu.make_async_copy(
                    source.at[:, cols], w.at[pl.ds(half * VOC, VOC), cols], w_sems.at[chunk, half]
                )
            )
    for copy in copies:
        copy.start()
    squares = norm_pieces(x, gain, xf, hid, normed)
    sums = jnp.sum(squares.T, axis=0, keepdims=True)
    inv = lax.rsqrt(sums * (1.0 / D) + 1e-05)
    unit_sketch = dot(table[RANK : 2 * RANK, :], hid[...], NT) * inv
    inv = inv * (RANK / D) ** 0.5
    aux[...] = dot(table[0:RANK, :], normed[...], NT) * (RANK / D) ** 0.5
    scores = logits[...]
    top = jnp.max(scores, axis=0, keepdims=True)
    rows = lax.broadcasted_iota(jnp.int32, (2 * VOC, LANES), 0)
    chosen = rows == hit[0:1, :]
    onehot = chosen.astype(f32)
    weights = jnp.exp(scores - top)
    others = jnp.where(chosen, 0.0, weights)
    at_target = jnp.sum(jnp.where(chosen, weights, 0.0), axis=0, keepdims=True)
    at_target_rows = jnp.broadcast_to(at_target, (LANES, LANES)).T
    high, low = split(others)
    left = jnp.concatenate(
        [others.T.astype(bf16), low.astype(f32).T.astype(bf16), onehot.T.astype(bf16)], axis=0
    )
    sums = jnp.zeros((RANK, 4 * TOK), f32)
    outs = []
    for chunk in range(chunks):
        copies[2 * chunk].wait()
        copies[2 * chunk + 1].wait()
        cols = slice(chunk * CHUNK, (chunk + 1) * CHUNK)
        both = dot(left, w[:, cols], NN)
        pick = both[2 * TOK :, :]
        full = both[0:TOK, :] + both[TOK : 2 * TOK, :]
        for k in range(CHUNK // LANES):
            lanes = slice(k * LANES, (k + 1) * LANES)
            place = slice(chunk * CHUNK + k * LANES, chunk * CHUNK + (k + 1) * LANES)
            soft[:, place] = full[:, lanes] + at_target_rows * pick[:, lanes]
        picked[:, cols] = pick.astype(bf16)
        spot = pl.ds(chunk * CHUNK, CHUNK)
        for sem, (source, target) in enumerate(((soft, soft_out), (picked, picked_out))):
            copy = pltpu.make_async_copy(
                source.at[:, spot], target.at[:, spot], out_sems.at[chunk, sem]
            )
            copy.start()
            outs.append(copy)
        full_high, full_low = split(soft[:, cols] * gain_row[:, cols])
        pick_high, pick_low = split(pick * gain_row[:, cols])
        right = jnp.concatenate([full_high, full_low, pick_high, pick_low], axis=0)
        sums = sums + dot(table[RANK : 2 * RANK, cols], right, NT)
    full_sketch = sums[:, 0:TOK] + sums[:, TOK : 2 * TOK]
    pick_sketch = sums[:, 2 * TOK : 3 * TOK] + sums[:, 3 * TOK :]
    full_mean = jnp.sum(weights * scores, axis=0, keepdims=True) * (1.0 / D)
    pick_mean = jnp.sum(onehot * scores, axis=0, keepdims=True) * (1.0 / D)
    signs = sign_rows(codes[...])
    pick_vocab = dot(signs, onehot.astype(bf16), NN)
    soft_vocab = dot(signs, high, NN) + dot(signs, low, NN) + at_target * pick_vocab
    columns[0:RANK, :] = soft_vocab
    columns[RANK : 2 * RANK, :] = pick_vocab
    columns[2 * RANK : 3 * RANK, :] = inv * (full_sketch - unit_sketch * full_mean)
    columns[3 * RANK : 4 * RANK, :] = inv * (pick_sketch - unit_sketch * pick_mean)
    columns[4 * RANK : 4 * RANK + 8, :] = jnp.broadcast_to(top, (8, LANES))
    for copy in outs:
        copy.wait()


def scale_kernel(stats, soft_in, picked_in, columns, blocks, df, soft, picked, sems):
    copies = []
    for chunk in range(D // CHUNK):
        cols = pl.ds(chunk * CHUNK, CHUNK)
        for sem, (source, target) in enumerate(((soft_in, soft), (picked_in, picked))):
            copy = pltpu.make_async_copy(
                source.at[:, cols], target.at[:, cols], sems.at[chunk, sem]
            )
            copy.start()
            copies.append(copy)
    tops = stats[pl.ds(0, PEERS, stride=4), :]
    totals = stats[pl.ds(1, PEERS, stride=4), :]
    acts = jnp.sum(stats[pl.ds(2, PEERS, stride=4), :], axis=0, keepdims=True)
    top = jnp.max(tops, axis=0, keepdims=True)
    denominator = jnp.sum(totals * jnp.exp(tops - top), axis=0, keepdims=True)
    scale = jnp.exp(columns[4 * RANK : 4 * RANK + 1, :] - top) / denominator
    scale_rows = jnp.broadcast_to(scale, (LANES, LANES)).T
    for k in range(PIECES):
        if k % (CHUNK // LANES) == 0:
            chunk = k // (CHUNK // LANES)
            copies[2 * chunk].wait()
            copies[2 * chunk + 1].wait()
        lanes = slice(k * LANES, (k + 1) * LANES)
        piece = scale_rows * soft[:, lanes] - picked[:, lanes].astype(f32)
        df[pl.ds(k, PEERS, stride=PITCH), :] = piece[0:PEERS, :]
        df[pl.ds(PIECES + k, PEERS, stride=PITCH), :] = piece[PEERS:TOK, :]
    vocab_sketch = scale * columns[0:RANK, :] - columns[RANK : 2 * RANK, :]
    grad_sketch = scale * columns[2 * RANK : 3 * RANK, :] - columns[3 * RANK : 4 * RANK, :]
    acts = jnp.broadcast_to(acts, (PEERS, LANES))
    for place, values in enumerate((vocab_sketch, grad_sketch, acts)):
        high = values.astype(bf16).astype(f32)
        df[pl.ds(2 * PIECES + 2 * place, PEERS, stride=PITCH), :] = high
        df[pl.ds(2 * PIECES + 2 * place + 1, PEERS, stride=PITCH), :] = values - high
    for row in (6, 7):
        df[pl.ds(2 * PIECES + row, PEERS, stride=PITCH), :] = jnp.zeros((PEERS, LANES), f32)
    blocks[...] = df[...].reshape(PEERS, PITCH, LANES).astype(bf16)


def feature_kernel(blocks, aux, docs, core, mine, other, rows):
    rows[...] = blocks[...].astype(f32)[:, 2 * PIECES :, :].reshape(PEERS * 8, LANES)

    def row(place):
        return rows[pl.ds(place, PEERS, stride=8), :]

    vocab_column = jnp.sum(row(0) + row(1), axis=0, keepdims=True)
    grad_column = jnp.sum(row(2) + row(3), axis=0, keepdims=True)
    acts = row(4) + row(5)
    act_sketch = jnp.concatenate([acts[:, 0:RANK], acts[:, RANK : 2 * RANK]], axis=0)
    act_sketch = act_sketch * (RANK / FF) ** 0.5
    ids = lax.broadcasted_iota(jnp.int32, (DOCS, LANES), 0)
    member = (docs[0:1, :] == ids).astype(f32)
    high = lax.Precision.HIGHEST
    head = dot(member * vocab_column, aux[...], NT, high)
    down = dot(member * grad_column, act_sketch, NN, high)
    both = jnp.concatenate([head, down], axis=0)
    first, second = both[:, 0 : RANK // 2], both[:, RANK // 2 :]
    is_first = core[0:1, 0:1] == 0
    mine[...] = jnp.where(is_first, first, second)
    other[...] = jnp.where(is_first, second, first)


def resid_kernel(blocks, hidden, gain, out):
    received = blocks[...].astype(f32)
    total = jnp.zeros((2 * PIECES, LANES), f32)
    for source in range(PEERS):
        total = total + received[source, 0 : 2 * PIECES, :]
    grads = []
    for token in range(2):
        rows = slice(token * PIECES, (token + 1) * PIECES)
        values = hidden[rows, :].astype(f32)
        inv = lax.rsqrt(jnp.sum(values * values, keepdims=True) * (1.0 / D) + 1e-05)
        unit = values * inv
        weighted = gain[...] * total[rows, :]
        inner = jnp.sum(weighted * unit, keepdims=True) * (1.0 / D)
        grads.append(inv * (weighted - unit * inner))
    for k in range(PIECES):
        pair = jnp.concatenate([grads[0][k : k + 1, :], grads[1][k : k + 1, :]], axis=0)
        out[:, k * LANES : (k + 1) * LANES] = pair.astype(bf16)


def shards(
    hidden,
    norm_gain,
    head_weight,
    gate_up,
    targets,
    doc_ids,
    vocab_codes,
    hidden_codes,
    model_codes,
):
    index = lax.axis_index("tensor")
    core = lax.rem(index, 2)
    groups = [list(range(0, 2 * PEERS, 2)), list(range(1, 2 * PEERS, 2))]
    partner = [(i, i ^ 1) for i in range(2 * PEERS)]
    gain32 = norm_gain.astype(f32)
    gain_row = gain32.reshape(1, D)
    gain_blk = gain32.reshape(PIECES, LANES)
    own_rows = hidden.reshape(2 * PIECES, LANES)

    def exchange(rows):
        return lax.all_to_all(rows, "tensor", 0, 0, axis_index_groups=groups, tiled=True)

    with jax.named_scope("gather_hidden"):
        spread = call(
            spread_kernel,
            jax.ShapeDtypeStruct((PEERS, 2 * PIECES, LANES), bf16),
            [],
            1,
            1000,
            MIB,
        )(hidden)
        gathered = exchange(spread).reshape(PEERS * 2 * PIECES, LANES)
    with jax.named_scope("partner_rows"):
        w_par = lax.ppermute(head_weight, "tensor", partner)
    with jax.named_scope("activations"):
        act_part = call(act_kernel, jax.ShapeDtypeStruct((RANK, 256), f32), [], 2, 8000000, 300000)(
            gate_up, hidden_codes.reshape(1, -1)
        )
        act_part = act_part.T.reshape(PEERS, 2, LANES)
        act_mine = lax.dynamic_index_in_dim(act_part, core, axis=1, keepdims=False)
        act_other = lax.dynamic_index_in_dim(act_part, 1 - core, axis=1, keepdims=False)
        codes_own = vocab_codes.astype(f32).reshape(VOC // LANES, LANES)
        sent = jnp.concatenate([act_other, codes_own], axis=0)
        came = lax.ppermute(sent, "tensor", partner)
        acts = act_mine + came[:PEERS]
        codes_par = came[PEERS:].astype(jnp.int32).reshape(1, VOC)
        codes = jnp.concatenate([vocab_codes.reshape(1, VOC), codes_par], axis=1)
    with jax.named_scope("tables"):
        table = call(
            table_kernel, jax.ShapeDtypeStruct((2 * RANK, D), bf16), [], 1, 4000000, 1100000
        )(model_codes)
        ids = jnp.stack([targets, doc_ids]).reshape(2, PEERS, 2, 2)
        ids = lax.dynamic_index_in_dim(ids, core, axis=2, keepdims=False)
        ids = ids.transpose(0, 2, 1).reshape(2, TOK)
        relative = ids[0] - index * VOC
        relative_par = ids[0] - (index + 1 - 2 * core) * VOC
        hit = jnp.where(
            (relative >= 0) & (relative < VOC),
            relative,
            jnp.where((relative_par >= 0) & (relative_par < VOC), relative_par + VOC, -1),
        ).reshape(1, TOK)
        docs = ids[1].reshape(1, TOK)
        core_row = jnp.full((1, LANES), core, jnp.int32)

    norm_scratch = [
        pltpu.VMEM((PEERS * PITCH, LANES), f32),
        pltpu.VMEM((TOK, D), bf16),
        pltpu.VMEM((TOK, D), bf16),
    ]
    with jax.named_scope("scores"):
        logits, payload = call(
            score_kernel,
            (
                jax.ShapeDtypeStruct((2 * VOC, TOK), f32),
                jax.ShapeDtypeStruct((PEERS * 4, LANES), f32),
            ),
            norm_scratch + [pltpu.VMEM((2 * VOC, D), bf16), pltpu.SemaphoreType.DMA((2,))],
            5,
            1 << 30,
            10 * MIB,
            any_inputs=(2, 3),
        )(gathered, gain_blk, head_weight, w_par, acts)
    with jax.named_scope("statistics"):
        stats = exchange(payload.reshape(PEERS, 4, LANES)).reshape(PEERS * 4, LANES)
    with jax.named_scope("backward"):
        soft, picked, columns, aux = call(
            backward_kernel,
            (
                jax.ShapeDtypeStruct((TOK, D), f32),
                jax.ShapeDtypeStruct((TOK, D), bf16),
                jax.ShapeDtypeStruct((4 * RANK + 8, LANES), f32),
                jax.ShapeDtypeStruct((RANK, LANES), f32),
            ),
            norm_scratch
            + [
                pltpu.VMEM((2 * VOC, D), bf16),
                pltpu.VMEM((TOK, D), f32),
                pltpu.VMEM((TOK, D), bf16),
                pltpu.SemaphoreType.DMA((D // CHUNK, 2)),
                pltpu.SemaphoreType.DMA((D // CHUNK, 2)),
            ],
            9,
            3 << 30,
            12 * MIB,
            any_inputs=(7, 8),
            any_outs=(0, 1),
        )(logits, hit, codes, table, gain_row, gathered, gain_blk, head_weight, w_par)
    with jax.named_scope("scale"):
        blocks = call(
            scale_kernel,
            jax.ShapeDtypeStruct((PEERS, PITCH, LANES), bf16),
            [
                pltpu.VMEM((PEERS * PITCH, LANES), f32),
                pltpu.VMEM((TOK, D), f32),
                pltpu.VMEM((TOK, D), bf16),
                pltpu.SemaphoreType.DMA((D // CHUNK, 2)),
            ],
            4,
            2000000,
            4 * MIB,
            any_inputs=(1, 2),
        )(stats, soft, picked, columns)
    with jax.named_scope("scatter_dnormed"):
        blocks, docs, core_row, gain_blk, aux, own_rows = lax.optimization_barrier(
            (blocks, docs, core_row, gain_blk, aux, own_rows)
        )
        received = exchange(blocks)
    with jax.named_scope("features"):
        half = jax.ShapeDtypeStruct((2 * DOCS, RANK // 2), f32)
        mine, other = call(
            feature_kernel,
            (half, half),
            [pltpu.VMEM((PEERS * 8, LANES), f32)],
            4,
            2000000,
            300000,
        )(received, aux, docs, core_row)
        features = mine + lax.ppermute(other, "tensor", partner)
    with jax.named_scope("resid_grad"):
        resid = call(
            resid_kernel,
            jax.ShapeDtypeStruct((2, D), bf16),
            [],
            3,
            2000000,
            MIB,
        )(received, own_rows, gain_blk)
    return resid, features[:DOCS], features[DOCS:]


def solution(mesh):
    in_specs = (
        P(("dp", "tensor"), None),
        P(),
        P("tensor", None),
        P(None, "tensor", "dp"),
        P("dp"),
        P("dp"),
        P("tensor"),
        P("tensor"),
        P(),
    )
    out_specs = (P(("dp", "tensor"), None), P("dp", "tensor"), P("dp", "tensor"))
    return jax.shard_map(shards, mesh=mesh, in_specs=in_specs, out_specs=out_specs, check_vma=False)
```

```python
import jax
import jax.numpy as jnp
from jax import lax
from jax.experimental import pallas as pl
from jax.experimental.pallas import tpu as pltpu
from jax.sharding import PartitionSpec as P

D = 4096
RANK = 64
DOCS = 8
PEERS = 64
TOK = 128
LANES = 128
PIECES = D // LANES
VOC = 512
FF = 28672
PITCH = 2 * PIECES + 8
CHUNK = 1024
PARTS = 4
MIB = 1 << 20

f32 = jnp.float32
bf16 = jnp.bfloat16

NN = (((1,), (0,)), ((), ()))
NT = (((1,), (1,)), ((), ()))
TN = (((0,), (0,)), ((), ()))


def dot(a, b, dims, precision=None):
    return lax.dot_general(a, b, dims, precision=precision, preferred_element_type=f32)


def sign_rows(codes_row):
    slots = lax.broadcasted_iota(jnp.int32, (RANK, codes_row.shape[1]), 0)
    plus = (codes_row == slots).astype(f32)
    minus = (codes_row == slots + RANK).astype(f32)
    return (plus - minus).astype(bf16)


def token_piece(ref, piece):
    first = ref[pl.ds(piece, PEERS, stride=PITCH), :]
    second = ref[pl.ds(PIECES + piece, PEERS, stride=PITCH), :]
    return jnp.concatenate([first, second], axis=0)


def call(kernel, outs, scratch, n_in, flops, bytes_accessed, any_inputs=(), any_outs=(), vmem=32 * MIB):
    specs = [
        pl.BlockSpec(memory_space=pltpu.HBM if i in any_inputs else pltpu.VMEM) for i in range(n_in)
    ]
    leaves, tree = jax.tree.flatten(outs)
    out_specs = tree.unflatten(
        [
            pl.BlockSpec(memory_space=pltpu.HBM if i in any_outs else pltpu.VMEM)
            for i in range(len(leaves))
        ]
    )
    leaves = [
        pltpu.HBM(leaf.shape, leaf.dtype) if i in any_outs else leaf
        for i, leaf in enumerate(leaves)
    ]
    inner = pl.pallas_call(
        kernel,
        out_shape=tree.unflatten(leaves),
        in_specs=specs,
        out_specs=out_specs,
        scratch_shapes=scratch,
        compiler_params=pltpu.CompilerParams(vmem_limit_bytes=vmem),
        cost_estimate=pl.CostEstimate(
            flops=flops, bytes_accessed=bytes_accessed, transcendentals=0
        ),
    )

    def run(*args):
        return inner(
            *[
                pltpu.with_memory_space_constraint(arg, pltpu.HBM) if i in any_inputs else arg
                for i, arg in enumerate(args)
            ]
        )

    return run


def spread_kernel(rows, out):
    pieces = [rows[:, k * LANES : (k + 1) * LANES].astype(f32) for k in range(PIECES)]
    stacked = jnp.concatenate([p[0:1, :] for p in pieces] + [p[1:2, :] for p in pieces], axis=0)
    stacked = stacked.astype(bf16)
    for peer in range(PEERS):
        out[peer, :, :] = stacked


def act_kernel(gate_up, codes, out):
    gate = gate_up[0].astype(f32)
    act = (gate / (1.0 + jnp.exp(-gate)) * gate_up[1].astype(f32)).astype(bf16)
    out[...] = dot(sign_rows(codes[...]), act, NN)


def table_kernel(codes, out):
    for block in range(8):
        cols = pl.ds(block * 512, 512)
        out[0:RANK, cols] = sign_rows(codes[0:1, cols])
        out[RANK : 2 * RANK, cols] = sign_rows(codes[1:2, cols])


def norm_pieces(x, gain, xf, hid, normed):
    for peer in range(PEERS):
        rows = slice(peer * 2 * PIECES, (peer + 1) * 2 * PIECES)
        xf[peer * PITCH : peer * PITCH + 2 * PIECES, :] = x[rows, :].astype(f32)
    squares = jnp.zeros((TOK, LANES), f32)
    for k in range(PIECES):
        piece = token_piece(xf, k)
        squares = squares + piece * piece
        hid[:, k * LANES : (k + 1) * LANES] = piece.astype(bf16)
    inv = lax.rsqrt(jnp.sum(squares, axis=1, keepdims=True) * (1.0 / D) + 1e-05)
    for k in range(PIECES):
        cols = slice(k * LANES, (k + 1) * LANES)
        unit = hid[:, cols].astype(f32) * inv
        normed[:, cols] = (unit * gain[k : k + 1, :]).astype(bf16)
    return squares


def score_kernel(x, gain, acts, w_own, *refs):
    w_par, (logits, payload, xf, hid, normed, w, sems) = refs[:PARTS], refs[PARTS:]
    size = VOC // PARTS
    copies = [[pltpu.make_async_copy(w_own, w.at[pl.ds(0, VOC)], sems.at[PARTS])], []]
    for part, source in enumerate(w_par):
        copies[1].append(
            pltpu.make_async_copy(source, w.at[pl.ds(VOC + part * size, size)], sems.at[part])
        )
    copies[0][0].start()
    norm_pieces(x, gain, xf, hid, normed)
    for copy in copies[1]:
        copy.start()
    for half in range(2):
        for copy in copies[half]:
            copy.wait()
        part = slice(half * VOC, (half + 1) * VOC)
        logits[part, :] = dot(normed[...], w[part, :], NT).T
    scores = logits[...]
    top = jnp.max(scores, axis=0, keepdims=True)
    total = jnp.sum(jnp.exp(scores - top), axis=0, keepdims=True)
    payload[pl.ds(0, PEERS, stride=4), :] = jnp.broadcast_to(top, (PEERS, LANES))
    payload[pl.ds(1, PEERS, stride=4), :] = jnp.broadcast_to(total, (PEERS, LANES))
    payload[pl.ds(2, PEERS, stride=4), :] = acts[...]
    payload[pl.ds(3, PEERS, stride=4), :] = jnp.zeros((PEERS, LANES), f32)


def split(values):
    high = values.astype(bf16)
    return high, (values - high.astype(f32)).astype(bf16)


def backward_kernel(logits, hit, codes, table, gain_row, x, gain, w_own, *refs):
    w_par, refs = refs[:PARTS], refs[PARTS:]
    soft_out, picked_out, columns, aux, xf, hid, normed, w, soft, picked, w_sems, out_sems = refs
    chunks = D // CHUNK
    size = VOC // PARTS
    copies = []
    for chunk in range(chunks):
        cols = pl.ds(chunk * CHUNK, CHUNK)
        sources = [(w_own, 0, VOC)]
        sources += [(source, VOC + part * size, size) for part, source in enumerate(w_par)]
        copies.append(
            [
                pltpu.make_async_copy(
                    source.at[:, cols], w.at[pl.ds(first, count), cols], w_sems.at[chunk, place]
                )
                for place, (source, first, count) in enumerate(sources)
            ]
        )
    for step in copies:
        for copy in step:
            copy.start()
    squares = norm_pieces(x, gain, xf, hid, normed)
    sums = jnp.sum(squares.T, axis=0, keepdims=True)
    inv = lax.rsqrt(sums * (1.0 / D) + 1e-05)
    unit_sketch = dot(table[RANK : 2 * RANK, :], hid[...], NT) * inv
    inv = inv * (RANK / D) ** 0.5
    aux[...] = dot(table[0:RANK, :], normed[...], NT) * (RANK / D) ** 0.5
    scores = logits[...]
    top = jnp.max(scores, axis=0, keepdims=True)
    rows = lax.broadcasted_iota(jnp.int32, (2 * VOC, LANES), 0)
    chosen = rows == hit[0:1, :]
    onehot = chosen.astype(f32)
    weights = jnp.exp(scores - top)
    others = jnp.where(chosen, 0.0, weights)
    at_target = jnp.sum(jnp.where(chosen, weights, 0.0), axis=0, keepdims=True)
    at_target_rows = jnp.broadcast_to(at_target, (LANES, LANES)).T
    high, low = split(others)
    left = jnp.concatenate(
        [others.T.astype(bf16), low.astype(f32).T.astype(bf16), onehot.T.astype(bf16)], axis=0
    )
    sums = jnp.zeros((RANK, 4 * TOK), f32)
    outs = []
    for chunk in range(chunks):
        for copy in copies[chunk]:
            copy.wait()
        cols = slice(chunk * CHUNK, (chunk + 1) * CHUNK)
        both = dot(left, w[:, cols], NN)
        pick = both[2 * TOK :, :]
        full = both[0:TOK, :] + both[TOK : 2 * TOK, :]
        for k in range(CHUNK // LANES):
            lanes = slice(k * LANES, (k + 1) * LANES)
            place = slice(chunk * CHUNK + k * LANES, chunk * CHUNK + (k + 1) * LANES)
            soft[:, place] = full[:, lanes] + at_target_rows * pick[:, lanes]
        picked[:, cols] = pick.astype(bf16)
        spot = pl.ds(chunk * CHUNK, CHUNK)
        for sem, (source, target) in enumerate(((soft, soft_out), (picked, picked_out))):
            copy = pltpu.make_async_copy(
                source.at[:, spot], target.at[:, spot], out_sems.at[chunk, sem]
            )
            copy.start()
            outs.append(copy)
        full_high, full_low = split(soft[:, cols] * gain_row[:, cols])
        pick_high, pick_low = split(pick * gain_row[:, cols])
        right = jnp.concatenate([full_high, full_low, pick_high, pick_low], axis=0)
        sums = sums + dot(table[RANK : 2 * RANK, cols], right, NT)
    full_sketch = sums[:, 0:TOK] + sums[:, TOK : 2 * TOK]
    pick_sketch = sums[:, 2 * TOK : 3 * TOK] + sums[:, 3 * TOK :]
    full_mean = jnp.sum(weights * scores, axis=0, keepdims=True) * (1.0 / D)
    pick_mean = jnp.sum(onehot * scores, axis=0, keepdims=True) * (1.0 / D)
    signs = sign_rows(codes[...])
    pick_vocab = dot(signs, onehot.astype(bf16), NN)
    soft_vocab = dot(signs, high, NN) + dot(signs, low, NN) + at_target * pick_vocab
    columns[0:RANK, :] = soft_vocab
    columns[RANK : 2 * RANK, :] = pick_vocab
    columns[2 * RANK : 3 * RANK, :] = inv * (full_sketch - unit_sketch * full_mean)
    columns[3 * RANK : 4 * RANK, :] = inv * (pick_sketch - unit_sketch * pick_mean)
    columns[4 * RANK : 4 * RANK + 8, :] = jnp.broadcast_to(top, (8, LANES))
    for copy in outs:
        copy.wait()


def scale_kernel(stats, soft_in, picked_in, columns, blocks, df, soft, picked, sems):
    copies = []
    for chunk in range(D // CHUNK):
        cols = pl.ds(chunk * CHUNK, CHUNK)
        for sem, (source, target) in enumerate(((soft_in, soft), (picked_in, picked))):
            copy = pltpu.make_async_copy(
                source.at[:, cols], target.at[:, cols], sems.at[chunk, sem]
            )
            copy.start()
            copies.append(copy)
    tops = stats[pl.ds(0, PEERS, stride=4), :]
    totals = stats[pl.ds(1, PEERS, stride=4), :]
    acts = jnp.sum(stats[pl.ds(2, PEERS, stride=4), :], axis=0, keepdims=True)
    top = jnp.max(tops, axis=0, keepdims=True)
    denominator = jnp.sum(totals * jnp.exp(tops - top), axis=0, keepdims=True)
    scale = jnp.exp(columns[4 * RANK : 4 * RANK + 1, :] - top) / denominator
    scale_rows = jnp.broadcast_to(scale, (LANES, LANES)).T
    for k in range(PIECES):
        if k % (CHUNK // LANES) == 0:
            chunk = k // (CHUNK // LANES)
            copies[2 * chunk].wait()
            copies[2 * chunk + 1].wait()
        lanes = slice(k * LANES, (k + 1) * LANES)
        piece = scale_rows * soft[:, lanes] - picked[:, lanes].astype(f32)
        df[pl.ds(k, PEERS, stride=PITCH), :] = piece[0:PEERS, :]
        df[pl.ds(PIECES + k, PEERS, stride=PITCH), :] = piece[PEERS:TOK, :]
    vocab_sketch = scale * columns[0:RANK, :] - columns[RANK : 2 * RANK, :]
    grad_sketch = scale * columns[2 * RANK : 3 * RANK, :] - columns[3 * RANK : 4 * RANK, :]
    acts = jnp.broadcast_to(acts, (PEERS, LANES))
    for place, values in enumerate((vocab_sketch, grad_sketch, acts)):
        high = values.astype(bf16).astype(f32)
        df[pl.ds(2 * PIECES + 2 * place, PEERS, stride=PITCH), :] = high
        df[pl.ds(2 * PIECES + 2 * place + 1, PEERS, stride=PITCH), :] = values - high
    for row in (6, 7):
        df[pl.ds(2 * PIECES + row, PEERS, stride=PITCH), :] = jnp.zeros((PEERS, LANES), f32)
    blocks[...] = df[...].reshape(PEERS, PITCH, LANES).astype(bf16)


def feature_kernel(blocks, aux, docs, core, mine, other, rows):
    rows[...] = blocks[...].astype(f32)[:, 2 * PIECES :, :].reshape(PEERS * 8, LANES)

    def row(place):
        return rows[pl.ds(place, PEERS, stride=8), :]

    vocab_column = jnp.sum(row(0) + row(1), axis=0, keepdims=True)
    grad_column = jnp.sum(row(2) + row(3), axis=0, keepdims=True)
    acts = row(4) + row(5)
    act_sketch = jnp.concatenate([acts[:, 0:RANK], acts[:, RANK : 2 * RANK]], axis=0)
    act_sketch = act_sketch * (RANK / FF) ** 0.5
    ids = lax.broadcasted_iota(jnp.int32, (DOCS, LANES), 0)
    member = (docs[0:1, :] == ids).astype(f32)
    high = lax.Precision.HIGHEST
    head = dot(member * vocab_column, aux[...], NT, high)
    down = dot(member * grad_column, act_sketch, NN, high)
    both = jnp.concatenate([head, down], axis=0)
    first, second = both[:, 0 : RANK // 2], both[:, RANK // 2 :]
    is_first = core[0:1, 0:1] == 0
    mine[...] = jnp.where(is_first, first, second)
    other[...] = jnp.where(is_first, second, first)


def resid_kernel(blocks, hidden, gain, out):
    received = blocks[...].astype(f32)
    total = jnp.zeros((2 * PIECES, LANES), f32)
    for source in range(PEERS):
        total = total + received[source, 0 : 2 * PIECES, :]
    grads = []
    for token in range(2):
        rows = slice(token * PIECES, (token + 1) * PIECES)
        values = hidden[rows, :].astype(f32)
        inv = lax.rsqrt(jnp.sum(values * values, keepdims=True) * (1.0 / D) + 1e-05)
        unit = values * inv
        weighted = gain[...] * total[rows, :]
        inner = jnp.sum(weighted * unit, keepdims=True) * (1.0 / D)
        grads.append(inv * (weighted - unit * inner))
    for k in range(PIECES):
        pair = jnp.concatenate([grads[0][k : k + 1, :], grads[1][k : k + 1, :]], axis=0)
        out[:, k * LANES : (k + 1) * LANES] = pair.astype(bf16)


def shards(
    hidden,
    norm_gain,
    head_weight,
    gate_up,
    targets,
    doc_ids,
    vocab_codes,
    hidden_codes,
    model_codes,
):
    index = lax.axis_index("tensor")
    core = lax.rem(index, 2)
    groups = [list(range(0, 2 * PEERS, 2)), list(range(1, 2 * PEERS, 2))]
    partner = [(i, i ^ 1) for i in range(2 * PEERS)]
    gain32 = norm_gain.astype(f32)
    gain_row = gain32.reshape(1, D)
    gain_blk = gain32.reshape(PIECES, LANES)
    own_rows = hidden.reshape(2 * PIECES, LANES)

    def exchange(rows):
        return lax.all_to_all(rows, "tensor", 0, 0, axis_index_groups=groups, tiled=True)

    with jax.named_scope("gather_hidden"):
        spread = call(
            spread_kernel,
            jax.ShapeDtypeStruct((PEERS, 2 * PIECES, LANES), bf16),
            [],
            1,
            1000,
            MIB,
        )(hidden)
        gathered = exchange(spread).reshape(PEERS * 2 * PIECES, LANES)
    with jax.named_scope("partner_rows"):
        size = VOC // PARTS
        w_par = [
            lax.ppermute(head_weight[part * size : (part + 1) * size], "tensor", partner)
            for part in range(PARTS)
        ]
    with jax.named_scope("activations"):
        act_part = call(act_kernel, jax.ShapeDtypeStruct((RANK, 256), f32), [], 2, 8000000, 300000)(
            gate_up, hidden_codes.reshape(1, -1)
        )
        act_part = act_part.T.reshape(PEERS, 2, LANES)
        act_mine = lax.dynamic_index_in_dim(act_part, core, axis=1, keepdims=False)
        act_other = lax.dynamic_index_in_dim(act_part, 1 - core, axis=1, keepdims=False)
        codes_own = vocab_codes.astype(f32).reshape(VOC // LANES, LANES)
        sent = jnp.concatenate([act_other, codes_own], axis=0)
        came = lax.ppermute(sent, "tensor", partner)
        acts = act_mine + came[:PEERS]
        codes_par = came[PEERS:].astype(jnp.int32).reshape(1, VOC)
        codes = jnp.concatenate([vocab_codes.reshape(1, VOC), codes_par], axis=1)
    with jax.named_scope("tables"):
        table = call(
            table_kernel, jax.ShapeDtypeStruct((2 * RANK, D), bf16), [], 1, 4000000, 1100000
        )(model_codes)
        ids = jnp.stack([targets, doc_ids]).reshape(2, PEERS, 2, 2)
        ids = lax.dynamic_index_in_dim(ids, core, axis=2, keepdims=False)
        ids = ids.transpose(0, 2, 1).reshape(2, TOK)
        relative = ids[0] - index * VOC
        relative_par = ids[0] - (index + 1 - 2 * core) * VOC
        hit = jnp.where(
            (relative >= 0) & (relative < VOC),
            relative,
            jnp.where((relative_par >= 0) & (relative_par < VOC), relative_par + VOC, -1),
        ).reshape(1, TOK)
        docs = ids[1].reshape(1, TOK)
        core_row = jnp.full((1, LANES), core, jnp.int32)

    norm_scratch = [
        pltpu.VMEM((PEERS * PITCH, LANES), f32),
        pltpu.VMEM((TOK, D), bf16),
        pltpu.VMEM((TOK, D), bf16),
    ]
    with jax.named_scope("scores"):
        logits, payload = call(
            score_kernel,
            (
                jax.ShapeDtypeStruct((2 * VOC, TOK), f32),
                jax.ShapeDtypeStruct((PEERS * 4, LANES), f32),
            ),
            norm_scratch + [pltpu.VMEM((2 * VOC, D), bf16), pltpu.SemaphoreType.DMA((PARTS + 1,))],
            4 + PARTS,
            1 << 30,
            10 * MIB,
            any_inputs=range(3, 4 + PARTS),
        )(gathered, gain_blk, acts, head_weight, *w_par)
    with jax.named_scope("statistics"):
        stats = exchange(payload.reshape(PEERS, 4, LANES)).reshape(PEERS * 4, LANES)
    with jax.named_scope("backward"):
        soft, picked, columns, aux = call(
            backward_kernel,
            (
                jax.ShapeDtypeStruct((TOK, D), f32),
                jax.ShapeDtypeStruct((TOK, D), bf16),
                jax.ShapeDtypeStruct((4 * RANK + 8, LANES), f32),
                jax.ShapeDtypeStruct((RANK, LANES), f32),
            ),
            norm_scratch
            + [
                pltpu.VMEM((2 * VOC, D), bf16),
                pltpu.VMEM((TOK, D), f32),
                pltpu.VMEM((TOK, D), bf16),
                pltpu.SemaphoreType.DMA((D // CHUNK, PARTS + 1)),
                pltpu.SemaphoreType.DMA((D // CHUNK, 2)),
            ],
            8 + PARTS,
            3 << 30,
            12 * MIB,
            any_inputs=range(7, 8 + PARTS),
            any_outs=(0, 1),
        )(logits, hit, codes, table, gain_row, gathered, gain_blk, head_weight, *w_par)
    with jax.named_scope("scale"):
        blocks = call(
            scale_kernel,
            jax.ShapeDtypeStruct((PEERS, PITCH, LANES), bf16),
            [
                pltpu.VMEM((PEERS * PITCH, LANES), f32),
                pltpu.VMEM((TOK, D), f32),
                pltpu.VMEM((TOK, D), bf16),
                pltpu.SemaphoreType.DMA((D // CHUNK, 2)),
            ],
            4,
            2000000,
            4 * MIB,
            any_inputs=(1, 2),
        )(stats, soft, picked, columns)
    with jax.named_scope("scatter_dnormed"):
        blocks, docs, core_row, gain_blk, aux, own_rows = lax.optimization_barrier(
            (blocks, docs, core_row, gain_blk, aux, own_rows)
        )
        received = exchange(blocks)
    with jax.named_scope("features"):
        half = jax.ShapeDtypeStruct((2 * DOCS, RANK // 2), f32)
        mine, other = call(
            feature_kernel,
            (half, half),
            [pltpu.VMEM((PEERS * 8, LANES), f32)],
            4,
            2000000,
            300000,
        )(received, aux, docs, core_row)
        features = mine + lax.ppermute(other, "tensor", partner)
    with jax.named_scope("resid_grad"):
        resid = call(
            resid_kernel,
            jax.ShapeDtypeStruct((2, D), bf16),
            [],
            3,
            2000000,
            MIB,
        )(received, own_rows, gain_blk)
    return resid, features[:DOCS], features[DOCS:]


def solution(mesh):
    in_specs = (
        P(("dp", "tensor"), None),
        P(),
        P("tensor", None),
        P(None, "tensor", "dp"),
        P("dp"),
        P("dp"),
        P("tensor"),
        P("tensor"),
        P(),
    )
    out_specs = (P(("dp", "tensor"), None), P("dp", "tensor"), P("dp", "tensor"))
    return jax.shard_map(shards, mesh=mesh, in_specs=in_specs, out_specs=out_specs, check_vma=False)
```

```python
import jax
import jax.numpy as jnp
from jax import lax
from jax.experimental import pallas as pl
from jax.experimental.pallas import tpu as pltpu
from jax.sharding import PartitionSpec as P

D = 4096
RANK = 64
DOCS = 8
PEERS = 64
TOK = 128
LANES = 128
PIECES = D // LANES
VOC = 512
FF = 28672
PITCH = 2 * PIECES + 8
CHUNK = 1024
PARTS = 4
MIB = 1 << 20

f32 = jnp.float32
bf16 = jnp.bfloat16

NN = (((1,), (0,)), ((), ()))
NT = (((1,), (1,)), ((), ()))
TN = (((0,), (0,)), ((), ()))


def dot(a, b, dims, precision=None):
    return lax.dot_general(a, b, dims, precision=precision, preferred_element_type=f32)


def sign_rows(codes_row):
    slots = lax.broadcasted_iota(jnp.int32, (RANK, codes_row.shape[1]), 0)
    plus = (codes_row == slots).astype(f32)
    minus = (codes_row == slots + RANK).astype(f32)
    return (plus - minus).astype(bf16)


def token_piece(ref, piece):
    first = ref[pl.ds(piece, PEERS, stride=PITCH), :]
    second = ref[pl.ds(PIECES + piece, PEERS, stride=PITCH), :]
    return jnp.concatenate([first, second], axis=0)


def call(kernel, outs, scratch, n_in, flops, bytes_accessed, any_inputs=(), any_outs=(), vmem=32 * MIB):
    specs = [
        pl.BlockSpec(memory_space=pltpu.HBM if i in any_inputs else pltpu.VMEM) for i in range(n_in)
    ]
    leaves, tree = jax.tree.flatten(outs)
    out_specs = tree.unflatten(
        [
            pl.BlockSpec(memory_space=pltpu.HBM if i in any_outs else pltpu.VMEM)
            for i in range(len(leaves))
        ]
    )
    leaves = [
        pltpu.HBM(leaf.shape, leaf.dtype) if i in any_outs else leaf
        for i, leaf in enumerate(leaves)
    ]
    inner = pl.pallas_call(
        kernel,
        out_shape=tree.unflatten(leaves),
        in_specs=specs,
        out_specs=out_specs,
        scratch_shapes=scratch,
        compiler_params=pltpu.CompilerParams(vmem_limit_bytes=vmem),
        cost_estimate=pl.CostEstimate(
            flops=flops, bytes_accessed=bytes_accessed, transcendentals=0
        ),
    )

    def run(*args):
        return inner(
            *[
                pltpu.with_memory_space_constraint(arg, pltpu.HBM) if i in any_inputs else arg
                for i, arg in enumerate(args)
            ]
        )

    return run


def spread_kernel(rows, out):
    pieces = [rows[:, k * LANES : (k + 1) * LANES].astype(f32) for k in range(PIECES)]
    stacked = jnp.concatenate([p[0:1, :] for p in pieces] + [p[1:2, :] for p in pieces], axis=0)
    stacked = stacked.astype(bf16)
    for peer in range(PEERS):
        out[peer, :, :] = stacked


def act_kernel(gate_up, codes, out):
    gate = gate_up[0].astype(f32)
    act = (gate / (1.0 + jnp.exp(-gate)) * gate_up[1].astype(f32)).astype(bf16)
    out[...] = dot(sign_rows(codes[...]), act, NN)


def table_kernel(codes, gain, out):
    for block in range(8):
        cols = pl.ds(block * 512, 512)
        out[0:RANK, cols] = sign_rows(codes[0:1, cols])
        signs = sign_rows(codes[1:2, cols])
        out[RANK : 2 * RANK, cols] = signs
        out[2 * RANK : 3 * RANK, cols] = (signs.astype(f32) * gain[:, cols]).astype(bf16)


def norm_pieces(x, gain, xf, hid, normed):
    for peer in range(PEERS):
        rows = slice(peer * 2 * PIECES, (peer + 1) * 2 * PIECES)
        xf[peer * PITCH : peer * PITCH + 2 * PIECES, :] = x[rows, :].astype(f32)
    squares = jnp.zeros((TOK, LANES), f32)
    for k in range(PIECES):
        piece = token_piece(xf, k)
        squares = squares + piece * piece
        hid[:, k * LANES : (k + 1) * LANES] = piece.astype(bf16)
    inv = lax.rsqrt(jnp.sum(squares, axis=1, keepdims=True) * (1.0 / D) + 1e-05)
    for k in range(PIECES):
        cols = slice(k * LANES, (k + 1) * LANES)
        unit = hid[:, cols].astype(f32) * inv
        normed[:, cols] = (unit * gain[k : k + 1, :]).astype(bf16)
    return squares


def score_kernel(x, gain, acts, w_own, *refs):
    w_par, (logits, payload, xf, hid, normed, w, sems) = refs[:PARTS], refs[PARTS:]
    size = VOC // PARTS
    copies = [[pltpu.make_async_copy(w_own, w.at[pl.ds(0, VOC)], sems.at[PARTS])], []]
    for part, source in enumerate(w_par):
        copies[1].append(
            pltpu.make_async_copy(source, w.at[pl.ds(VOC + part * size, size)], sems.at[part])
        )
    copies[0][0].start()
    norm_pieces(x, gain, xf, hid, normed)
    for copy in copies[1]:
        copy.start()
    for half in range(2):
        for copy in copies[half]:
            copy.wait()
        part = slice(half * VOC, (half + 1) * VOC)
        logits[part, :] = dot(normed[...], w[part, :], NT).T
    scores = logits[...]
    top = jnp.max(scores, axis=0, keepdims=True)
    total = jnp.sum(jnp.exp(scores - top), axis=0, keepdims=True)
    payload[pl.ds(0, PEERS, stride=4), :] = jnp.broadcast_to(top, (PEERS, LANES))
    payload[pl.ds(1, PEERS, stride=4), :] = jnp.broadcast_to(total, (PEERS, LANES))
    payload[pl.ds(2, PEERS, stride=4), :] = acts[...]
    payload[pl.ds(3, PEERS, stride=4), :] = jnp.zeros((PEERS, LANES), f32)


def split(values):
    high = values.astype(bf16)
    return high, (values - high.astype(f32)).astype(bf16)


def backward_kernel(logits, hit, codes, table, x, gain, w_own, *refs):
    w_par, refs = refs[:PARTS], refs[PARTS:]
    soft_out, picked_out, columns, aux, xf, hid, normed, w, soft, picked, w_sems, out_sems = refs
    chunks = D // CHUNK
    size = VOC // PARTS
    copies = []
    for chunk in range(chunks):
        cols = pl.ds(chunk * CHUNK, CHUNK)
        sources = [(w_own, 0, VOC)]
        sources += [(source, VOC + part * size, size) for part, source in enumerate(w_par)]
        copies.append(
            [
                pltpu.make_async_copy(
                    source.at[:, cols], w.at[pl.ds(first, count), cols], w_sems.at[chunk, place]
                )
                for place, (source, first, count) in enumerate(sources)
            ]
        )
    for step in copies:
        for copy in step:
            copy.start()
    squares = norm_pieces(x, gain, xf, hid, normed)
    sums = jnp.sum(squares.T, axis=0, keepdims=True)
    inv = lax.rsqrt(sums * (1.0 / D) + 1e-05)
    unit_sketch = dot(table[RANK : 2 * RANK, :], hid[...], NT) * inv
    inv = inv * (RANK / D) ** 0.5
    aux[...] = dot(table[0:RANK, :], normed[...], NT) * (RANK / D) ** 0.5
    scores = logits[...]
    top = jnp.max(scores, axis=0, keepdims=True)
    rows = lax.broadcasted_iota(jnp.int32, (2 * VOC, LANES), 0)
    chosen = rows == hit[0:1, :]
    onehot = chosen.astype(f32)
    weights = jnp.exp(scores - top)
    others = jnp.where(chosen, 0.0, weights)
    at_target = jnp.sum(jnp.where(chosen, weights, 0.0), axis=0, keepdims=True)
    at_target_rows = jnp.broadcast_to(at_target, (LANES, LANES)).T
    high, low = split(others)
    left = jnp.concatenate(
        [others.T.astype(bf16), low.astype(f32).T.astype(bf16), onehot.T.astype(bf16)], axis=0
    )
    sums = jnp.zeros((RANK, 3 * TOK), f32)
    outs = []
    for chunk in range(chunks):
        for copy in copies[chunk]:
            copy.wait()
        cols = slice(chunk * CHUNK, (chunk + 1) * CHUNK)
        both = dot(left, w[:, cols], NN)
        pick = both[2 * TOK :, :]
        full = both[0:TOK, :] + both[TOK : 2 * TOK, :]
        for k in range(CHUNK // LANES):
            lanes = slice(k * LANES, (k + 1) * LANES)
            place = slice(chunk * CHUNK + k * LANES, chunk * CHUNK + (k + 1) * LANES)
            soft[:, place] = full[:, lanes] + at_target_rows * pick[:, lanes]
        picked[:, cols] = pick.astype(bf16)
        spot = pl.ds(chunk * CHUNK, CHUNK)
        for sem, (source, target) in enumerate(((soft, soft_out), (picked, picked_out))):
            copy = pltpu.make_async_copy(
                source.at[:, spot], target.at[:, spot], out_sems.at[chunk, sem]
            )
            copy.start()
            outs.append(copy)
        full_high, full_low = split(soft[:, cols])
        right = jnp.concatenate([full_high, full_low, pick.astype(bf16)], axis=0)
        sums = sums + dot(table[2 * RANK : 3 * RANK, cols], right, NT)
    full_sketch = sums[:, 0:TOK] + sums[:, TOK : 2 * TOK]
    pick_sketch = sums[:, 2 * TOK :]
    full_mean = jnp.sum(weights * scores, axis=0, keepdims=True) * (1.0 / D)
    pick_mean = jnp.sum(onehot * scores, axis=0, keepdims=True) * (1.0 / D)
    signs = sign_rows(codes[...])
    pick_vocab = dot(signs, onehot.astype(bf16), NN)
    soft_vocab = dot(signs, high, NN) + dot(signs, low, NN) + at_target * pick_vocab
    columns[0:RANK, :] = soft_vocab
    columns[RANK : 2 * RANK, :] = pick_vocab
    columns[2 * RANK : 3 * RANK, :] = inv * (full_sketch - unit_sketch * full_mean)
    columns[3 * RANK : 4 * RANK, :] = inv * (pick_sketch - unit_sketch * pick_mean)
    columns[4 * RANK : 4 * RANK + 8, :] = jnp.broadcast_to(top, (8, LANES))
    for copy in outs:
        copy.wait()


def scale_kernel(stats, soft_in, picked_in, columns, blocks, df, soft, picked, sems):
    copies = []
    for chunk in range(D // CHUNK):
        cols = pl.ds(chunk * CHUNK, CHUNK)
        for sem, (source, target) in enumerate(((soft_in, soft), (picked_in, picked))):
            copy = pltpu.make_async_copy(
                source.at[:, cols], target.at[:, cols], sems.at[chunk, sem]
            )
            copy.start()
            copies.append(copy)
    tops = stats[pl.ds(0, PEERS, stride=4), :]
    totals = stats[pl.ds(1, PEERS, stride=4), :]
    acts = jnp.sum(stats[pl.ds(2, PEERS, stride=4), :], axis=0, keepdims=True)
    top = jnp.max(tops, axis=0, keepdims=True)
    denominator = jnp.sum(totals * jnp.exp(tops - top), axis=0, keepdims=True)
    scale = jnp.exp(columns[4 * RANK : 4 * RANK + 1, :] - top) / denominator
    scale_rows = jnp.broadcast_to(scale, (LANES, LANES)).T
    for k in range(PIECES):
        if k % (CHUNK // LANES) == 0:
            chunk = k // (CHUNK // LANES)
            copies[2 * chunk].wait()
            copies[2 * chunk + 1].wait()
        lanes = slice(k * LANES, (k + 1) * LANES)
        piece = scale_rows * soft[:, lanes] - picked[:, lanes].astype(f32)
        df[pl.ds(k, PEERS, stride=PITCH), :] = piece[0:PEERS, :]
        df[pl.ds(PIECES + k, PEERS, stride=PITCH), :] = piece[PEERS:TOK, :]
    vocab_sketch = scale * columns[0:RANK, :] - columns[RANK : 2 * RANK, :]
    grad_sketch = scale * columns[2 * RANK : 3 * RANK, :] - columns[3 * RANK : 4 * RANK, :]
    acts = jnp.broadcast_to(acts, (PEERS, LANES))
    for place, values in enumerate((vocab_sketch, grad_sketch, acts)):
        high = values.astype(bf16).astype(f32)
        df[pl.ds(2 * PIECES + 2 * place, PEERS, stride=PITCH), :] = high
        df[pl.ds(2 * PIECES + 2 * place + 1, PEERS, stride=PITCH), :] = values - high
    for row in (6, 7):
        df[pl.ds(2 * PIECES + row, PEERS, stride=PITCH), :] = jnp.zeros((PEERS, LANES), f32)
    blocks[...] = df[...].reshape(PEERS, PITCH, LANES).astype(bf16)


def feature_kernel(blocks, aux, docs, core, mine, other, rows):
    rows[...] = blocks[...].astype(f32)[:, 2 * PIECES :, :].reshape(PEERS * 8, LANES)

    def row(place):
        return rows[pl.ds(place, PEERS, stride=8), :]

    vocab_column = jnp.sum(row(0) + row(1), axis=0, keepdims=True)
    grad_column = jnp.sum(row(2) + row(3), axis=0, keepdims=True)
    acts = row(4) + row(5)
    act_sketch = jnp.concatenate([acts[:, 0:RANK], acts[:, RANK : 2 * RANK]], axis=0)
    act_sketch = act_sketch * (RANK / FF) ** 0.5
    ids = lax.broadcasted_iota(jnp.int32, (DOCS, LANES), 0)
    member = (docs[0:1, :] == ids).astype(f32)
    high = lax.Precision.HIGHEST
    head = dot(member * vocab_column, aux[...], NT, high)
    down = dot(member * grad_column, act_sketch, NN, high)
    both = jnp.concatenate([head, down], axis=0)
    first, second = both[:, 0 : RANK // 2], both[:, RANK // 2 :]
    is_first = core[0:1, 0:1] == 0
    mine[...] = jnp.where(is_first, first, second)
    other[...] = jnp.where(is_first, second, first)


def resid_kernel(blocks, hidden, gain, out):
    received = blocks[...].astype(f32)
    total = jnp.zeros((2 * PIECES, LANES), f32)
    for source in range(PEERS):
        total = total + received[source, 0 : 2 * PIECES, :]
    grads = []
    for token in range(2):
        rows = slice(token * PIECES, (token + 1) * PIECES)
        values = hidden[rows, :].astype(f32)
        inv = lax.rsqrt(jnp.sum(values * values, keepdims=True) * (1.0 / D) + 1e-05)
        unit = values * inv
        weighted = gain[...] * total[rows, :]
        inner = jnp.sum(weighted * unit, keepdims=True) * (1.0 / D)
        grads.append(inv * (weighted - unit * inner))
    for k in range(PIECES):
        pair = jnp.concatenate([grads[0][k : k + 1, :], grads[1][k : k + 1, :]], axis=0)
        out[:, k * LANES : (k + 1) * LANES] = pair.astype(bf16)


def shards(
    hidden,
    norm_gain,
    head_weight,
    gate_up,
    targets,
    doc_ids,
    vocab_codes,
    hidden_codes,
    model_codes,
):
    index = lax.axis_index("tensor")
    core = lax.rem(index, 2)
    groups = [list(range(0, 2 * PEERS, 2)), list(range(1, 2 * PEERS, 2))]
    partner = [(i, i ^ 1) for i in range(2 * PEERS)]
    gain32 = norm_gain.astype(f32)
    gain_row = gain32.reshape(1, D)
    gain_blk = gain32.reshape(PIECES, LANES)
    own_rows = hidden.reshape(2 * PIECES, LANES)

    def exchange(rows):
        return lax.all_to_all(rows, "tensor", 0, 0, axis_index_groups=groups, tiled=True)

    with jax.named_scope("gather_hidden"):
        spread = call(
            spread_kernel,
            jax.ShapeDtypeStruct((PEERS, 2 * PIECES, LANES), bf16),
            [],
            1,
            1000,
            MIB,
        )(hidden)
        gathered = exchange(spread).reshape(PEERS * 2 * PIECES, LANES)
    with jax.named_scope("partner_rows"):
        size = VOC // PARTS
        w_par = [
            lax.ppermute(head_weight[part * size : (part + 1) * size], "tensor", partner)
            for part in range(PARTS)
        ]
    with jax.named_scope("activations"):
        act_part = call(act_kernel, jax.ShapeDtypeStruct((RANK, 256), f32), [], 2, 8000000, 300000)(
            gate_up, hidden_codes.reshape(1, -1)
        )
        act_part = act_part.T.reshape(PEERS, 2, LANES)
        act_mine = lax.dynamic_index_in_dim(act_part, core, axis=1, keepdims=False)
        act_other = lax.dynamic_index_in_dim(act_part, 1 - core, axis=1, keepdims=False)
        codes_own = vocab_codes.astype(f32).reshape(VOC // LANES, LANES)
        sent = jnp.concatenate([act_other, codes_own], axis=0)
        came = lax.ppermute(sent, "tensor", partner)
        acts = act_mine + came[:PEERS]
        codes_par = came[PEERS:].astype(jnp.int32).reshape(1, VOC)
        codes = jnp.concatenate([vocab_codes.reshape(1, VOC), codes_par], axis=1)
    with jax.named_scope("tables"):
        table = call(
            table_kernel, jax.ShapeDtypeStruct((3 * RANK, D), bf16), [], 2, 4000000, 1600000
        )(model_codes, gain_row)
        ids = jnp.stack([targets, doc_ids]).reshape(2, PEERS, 2, 2)
        ids = lax.dynamic_index_in_dim(ids, core, axis=2, keepdims=False)
        ids = ids.transpose(0, 2, 1).reshape(2, TOK)
        relative = ids[0] - index * VOC
        relative_par = ids[0] - (index + 1 - 2 * core) * VOC
        hit = jnp.where(
            (relative >= 0) & (relative < VOC),
            relative,
            jnp.where((relative_par >= 0) & (relative_par < VOC), relative_par + VOC, -1),
        ).reshape(1, TOK)
        docs = ids[1].reshape(1, TOK)
        core_row = jnp.full((1, LANES), core, jnp.int32)

    norm_scratch = [
        pltpu.VMEM((PEERS * PITCH, LANES), f32),
        pltpu.VMEM((TOK, D), bf16),
        pltpu.VMEM((TOK, D), bf16),
    ]
    with jax.named_scope("scores"):
        logits, payload = call(
            score_kernel,
            (
                jax.ShapeDtypeStruct((2 * VOC, TOK), f32),
                jax.ShapeDtypeStruct((PEERS * 4, LANES), f32),
            ),
            norm_scratch + [pltpu.VMEM((2 * VOC, D), bf16), pltpu.SemaphoreType.DMA((PARTS + 1,))],
            4 + PARTS,
            1 << 30,
            10 * MIB,
            any_inputs=range(3, 4 + PARTS),
        )(gathered, gain_blk, acts, head_weight, *w_par)
    with jax.named_scope("statistics"):
        stats = exchange(payload.reshape(PEERS, 4, LANES)).reshape(PEERS * 4, LANES)
    with jax.named_scope("backward"):
        soft, picked, columns, aux = call(
            backward_kernel,
            (
                jax.ShapeDtypeStruct((TOK, D), f32),
                jax.ShapeDtypeStruct((TOK, D), bf16),
                jax.ShapeDtypeStruct((4 * RANK + 8, LANES), f32),
                jax.ShapeDtypeStruct((RANK, LANES), f32),
            ),
            norm_scratch
            + [
                pltpu.VMEM((2 * VOC, D), bf16),
                pltpu.VMEM((TOK, D), f32),
                pltpu.VMEM((TOK, D), bf16),
                pltpu.SemaphoreType.DMA((D // CHUNK, PARTS + 1)),
                pltpu.SemaphoreType.DMA((D // CHUNK, 2)),
            ],
            7 + PARTS,
            3 << 30,
            12 * MIB,
            any_inputs=range(6, 7 + PARTS),
            any_outs=(0, 1),
        )(logits, hit, codes, table, gathered, gain_blk, head_weight, *w_par)
    with jax.named_scope("scale"):
        blocks = call(
            scale_kernel,
            jax.ShapeDtypeStruct((PEERS, PITCH, LANES), bf16),
            [
                pltpu.VMEM((PEERS * PITCH, LANES), f32),
                pltpu.VMEM((TOK, D), f32),
                pltpu.VMEM((TOK, D), bf16),
                pltpu.SemaphoreType.DMA((D // CHUNK, 2)),
            ],
            4,
            2000000,
            4 * MIB,
            any_inputs=(1, 2),
        )(stats, soft, picked, columns)
    with jax.named_scope("scatter_dnormed"):
        blocks, docs, core_row, gain_blk, aux, own_rows = lax.optimization_barrier(
            (blocks, docs, core_row, gain_blk, aux, own_rows)
        )
        received = exchange(blocks)
    with jax.named_scope("features"):
        half = jax.ShapeDtypeStruct((2 * DOCS, RANK // 2), f32)
        mine, other = call(
            feature_kernel,
            (half, half),
            [pltpu.VMEM((PEERS * 8, LANES), f32)],
            4,
            2000000,
            300000,
        )(received, aux, docs, core_row)
        features = mine + lax.ppermute(other, "tensor", partner)
    with jax.named_scope("resid_grad"):
        resid = call(
            resid_kernel,
            jax.ShapeDtypeStruct((2, D), bf16),
            [],
            3,
            2000000,
            MIB,
        )(received, own_rows, gain_blk)
    return resid, features[:DOCS], features[DOCS:]


def solution(mesh):
    in_specs = (
        P(("dp", "tensor"), None),
        P(),
        P("tensor", None),
        P(None, "tensor", "dp"),
        P("dp"),
        P("dp"),
        P("tensor"),
        P("tensor"),
        P(),
    )
    out_specs = (P(("dp", "tensor"), None), P("dp", "tensor"), P("dp", "tensor"))
    return jax.shard_map(shards, mesh=mesh, in_specs=in_specs, out_specs=out_specs, check_vma=False)
```

```python
import jax
import jax.numpy as jnp
from jax import lax
from jax.experimental import pallas as pl
from jax.experimental.pallas import tpu as pltpu
from jax.sharding import PartitionSpec as P

D = 4096
RANK = 64
DOCS = 8
PEERS = 64
TOK = 128
LANES = 128
PIECES = D // LANES
VOC = 512
FF = 28672
PITCH = 2 * PIECES + 8
CHUNK = 1024
PARTS = 4
MIB = 1 << 20

f32 = jnp.float32
bf16 = jnp.bfloat16

NN = (((1,), (0,)), ((), ()))
NT = (((1,), (1,)), ((), ()))
TN = (((0,), (0,)), ((), ()))


def dot(a, b, dims, precision=None):
    return lax.dot_general(a, b, dims, precision=precision, preferred_element_type=f32)


def sign_rows(codes_row):
    slots = lax.broadcasted_iota(jnp.int32, (RANK, codes_row.shape[1]), 0)
    plus = (codes_row == slots).astype(f32)
    minus = (codes_row == slots + RANK).astype(f32)
    return (plus - minus).astype(bf16)


def token_piece(ref, piece):
    first = ref[pl.ds(piece, PEERS, stride=PITCH), :]
    second = ref[pl.ds(PIECES + piece, PEERS, stride=PITCH), :]
    return jnp.concatenate([first, second], axis=0)


def call(kernel, outs, scratch, n_in, flops, bytes_accessed, any_inputs=(), any_outs=(), vmem=32 * MIB):
    specs = [
        pl.BlockSpec(memory_space=pltpu.HBM if i in any_inputs else pltpu.VMEM) for i in range(n_in)
    ]
    leaves, tree = jax.tree.flatten(outs)
    out_specs = tree.unflatten(
        [
            pl.BlockSpec(memory_space=pltpu.HBM if i in any_outs else pltpu.VMEM)
            for i in range(len(leaves))
        ]
    )
    leaves = [
        pltpu.HBM(leaf.shape, leaf.dtype) if i in any_outs else leaf
        for i, leaf in enumerate(leaves)
    ]
    inner = pl.pallas_call(
        kernel,
        out_shape=tree.unflatten(leaves),
        in_specs=specs,
        out_specs=out_specs,
        scratch_shapes=scratch,
        compiler_params=pltpu.CompilerParams(vmem_limit_bytes=vmem),
        cost_estimate=pl.CostEstimate(
            flops=flops, bytes_accessed=bytes_accessed, transcendentals=0
        ),
    )

    def run(*args):
        return inner(
            *[
                pltpu.with_memory_space_constraint(arg, pltpu.HBM) if i in any_inputs else arg
                for i, arg in enumerate(args)
            ]
        )

    return run


def spread_kernel(rows, out):
    pieces = [rows[:, k * LANES : (k + 1) * LANES].astype(f32) for k in range(PIECES)]
    stacked = jnp.concatenate([p[0:1, :] for p in pieces] + [p[1:2, :] for p in pieces], axis=0)
    stacked = stacked.astype(bf16)
    for peer in range(PEERS):
        out[peer, :, :] = stacked


def act_kernel(gate_up, codes, out):
    gate = gate_up[0].astype(f32)
    act = (gate / (1.0 + jnp.exp(-gate)) * gate_up[1].astype(f32)).astype(bf16)
    out[...] = dot(sign_rows(codes[...]), act, NN)


def table_kernel(codes, gain, out):
    for block in range(8):
        cols = pl.ds(block * 512, 512)
        out[0:RANK, cols] = sign_rows(codes[0:1, cols])
        signs = sign_rows(codes[1:2, cols])
        out[RANK : 2 * RANK, cols] = signs
        out[2 * RANK : 3 * RANK, cols] = (signs.astype(f32) * gain[:, cols]).astype(bf16)


def norm_pieces(x, gain, xf, hid, normed):
    for peer in range(PEERS):
        rows = slice(peer * 2 * PIECES, (peer + 1) * 2 * PIECES)
        xf[peer * PITCH : peer * PITCH + 2 * PIECES, :] = x[rows, :].astype(f32)
    squares = jnp.zeros((TOK, LANES), f32)
    for k in range(PIECES):
        piece = token_piece(xf, k)
        squares = squares + piece * piece
        hid[:, k * LANES : (k + 1) * LANES] = piece.astype(bf16)
    inv = lax.rsqrt(jnp.sum(squares, axis=1, keepdims=True) * (1.0 / D) + 1e-05)
    for k in range(PIECES):
        cols = slice(k * LANES, (k + 1) * LANES)
        unit = hid[:, cols].astype(f32) * inv
        normed[:, cols] = (unit * gain[k : k + 1, :]).astype(bf16)
    return squares


def score_kernel(x, gain, acts, w_own, *refs):
    w_par, (logits, payload, xf, hid, normed, w, sems) = refs[:PARTS], refs[PARTS:]
    size = VOC // PARTS
    copies = [[pltpu.make_async_copy(w_own, w.at[pl.ds(0, VOC)], sems.at[PARTS])], []]
    for part, source in enumerate(w_par):
        copies[1].append(
            pltpu.make_async_copy(source, w.at[pl.ds(VOC + part * size, size)], sems.at[part])
        )
    copies[0][0].start()
    norm_pieces(x, gain, xf, hid, normed)
    for copy in copies[1]:
        copy.start()
    for half in range(2):
        for copy in copies[half]:
            copy.wait()
        part = slice(half * VOC, (half + 1) * VOC)
        logits[part, :] = dot(normed[...], w[part, :], NT).T
    scores = logits[...]
    top = jnp.max(scores, axis=0, keepdims=True)
    total = jnp.sum(jnp.exp(scores - top), axis=0, keepdims=True)
    payload[pl.ds(0, PEERS, stride=4), :] = jnp.broadcast_to(top, (PEERS, LANES))
    payload[pl.ds(1, PEERS, stride=4), :] = jnp.broadcast_to(total, (PEERS, LANES))
    payload[pl.ds(2, PEERS, stride=4), :] = acts[...]
    payload[pl.ds(3, PEERS, stride=4), :] = jnp.zeros((PEERS, LANES), f32)


def split(values):
    high = values.astype(bf16)
    return high, (values - high.astype(f32)).astype(bf16)


def backward_kernel(logits, hit, codes, table, x, gain, w_own, *refs):
    w_par, refs = refs[:PARTS], refs[PARTS:]
    soft_out, picked_out, columns, aux, xf, hid, normed, w, soft, picked, w_sems, out_sems = refs
    chunks = D // CHUNK
    size = VOC // PARTS
    copies = []
    for chunk in range(chunks):
        cols = pl.ds(chunk * CHUNK, CHUNK)
        sources = [(w_own, 0, VOC)]
        sources += [(source, VOC + part * size, size) for part, source in enumerate(w_par)]
        copies.append(
            [
                pltpu.make_async_copy(
                    source.at[:, cols], w.at[pl.ds(first, count), cols], w_sems.at[chunk, place]
                )
                for place, (source, first, count) in enumerate(sources)
            ]
        )
    for step in copies:
        for copy in step:
            copy.start()
    squares = norm_pieces(x, gain, xf, hid, normed)
    sums = jnp.sum(squares.T, axis=0, keepdims=True)
    inv = lax.rsqrt(sums * (1.0 / D) + 1e-05)
    unit_sketch = dot(table[RANK : 2 * RANK, :], hid[...], NT) * inv
    inv = inv * (RANK / D) ** 0.5
    aux[...] = dot(table[0:RANK, :], normed[...], NT) * (RANK / D) ** 0.5
    scores = logits[...]
    top = jnp.max(scores, axis=0, keepdims=True)
    rows = lax.broadcasted_iota(jnp.int32, (2 * VOC, LANES), 0)
    chosen = rows == hit[0:1, :]
    onehot = chosen.astype(f32)
    weights = jnp.exp(scores - top)
    others = jnp.where(chosen, 0.0, weights)
    at_target = jnp.sum(jnp.where(chosen, weights, 0.0), axis=0, keepdims=True)
    high, low = split(others)
    left = jnp.concatenate(
        [others.T.astype(bf16), low.astype(f32).T.astype(bf16), onehot.T.astype(bf16)], axis=0
    )
    sums = jnp.zeros((RANK, 3 * TOK), f32)
    outs = []
    for chunk in range(chunks):
        for copy in copies[chunk]:
            copy.wait()
        cols = slice(chunk * CHUNK, (chunk + 1) * CHUNK)
        both = dot(left, w[:, cols], NN)
        pick = both[2 * TOK :, :]
        full = both[0:TOK, :] + both[TOK : 2 * TOK, :]
        soft[:, cols] = full
        picked[:, cols] = pick.astype(bf16)
        spot = pl.ds(chunk * CHUNK, CHUNK)
        for sem, (source, target) in enumerate(((soft, soft_out), (picked, picked_out))):
            copy = pltpu.make_async_copy(
                source.at[:, spot], target.at[:, spot], out_sems.at[chunk, sem]
            )
            copy.start()
            outs.append(copy)
        full_high, full_low = split(full)
        right = jnp.concatenate([full_high, full_low, pick.astype(bf16)], axis=0)
        sums = sums + dot(table[2 * RANK : 3 * RANK, cols], right, NT)
    full_sketch = sums[:, 0:TOK] + sums[:, TOK : 2 * TOK]
    pick_sketch = sums[:, 2 * TOK :]
    full_mean = jnp.sum(others * scores, axis=0, keepdims=True) * (1.0 / D)
    pick_mean = jnp.sum(onehot * scores, axis=0, keepdims=True) * (1.0 / D)
    signs = sign_rows(codes[...])
    pick_vocab = dot(signs, onehot.astype(bf16), NN)
    soft_vocab = dot(signs, high, NN) + dot(signs, low, NN)
    columns[0:RANK, :] = soft_vocab
    columns[RANK : 2 * RANK, :] = pick_vocab
    columns[2 * RANK : 3 * RANK, :] = inv * (full_sketch - unit_sketch * full_mean)
    columns[3 * RANK : 4 * RANK, :] = inv * (pick_sketch - unit_sketch * pick_mean)
    columns[4 * RANK : 4 * RANK + 8, :] = jnp.broadcast_to(top, (8, LANES))
    columns[4 * RANK + 8 : 4 * RANK + 16, :] = jnp.broadcast_to(at_target, (8, LANES))
    for copy in outs:
        copy.wait()


def scale_kernel(stats, soft_in, picked_in, columns, blocks, df, soft, picked, sems):
    copies = []
    for chunk in range(D // CHUNK):
        cols = pl.ds(chunk * CHUNK, CHUNK)
        for sem, (source, target) in enumerate(((soft_in, soft), (picked_in, picked))):
            copy = pltpu.make_async_copy(
                source.at[:, cols], target.at[:, cols], sems.at[chunk, sem]
            )
            copy.start()
            copies.append(copy)
    tops = stats[pl.ds(0, PEERS, stride=4), :]
    totals = stats[pl.ds(1, PEERS, stride=4), :]
    acts = jnp.sum(stats[pl.ds(2, PEERS, stride=4), :], axis=0, keepdims=True)
    top = jnp.max(tops, axis=0, keepdims=True)
    denominator = jnp.sum(totals * jnp.exp(tops - top), axis=0, keepdims=True)
    scale = jnp.exp(columns[4 * RANK : 4 * RANK + 1, :] - top) / denominator
    target = scale * columns[4 * RANK + 8 : 4 * RANK + 9, :] - 1.0
    scale_rows = jnp.broadcast_to(scale, (LANES, LANES)).T
    target_rows = jnp.broadcast_to(target, (LANES, LANES)).T
    for k in range(PIECES):
        if k % (CHUNK // LANES) == 0:
            chunk = k // (CHUNK // LANES)
            copies[2 * chunk].wait()
            copies[2 * chunk + 1].wait()
        lanes = slice(k * LANES, (k + 1) * LANES)
        piece = scale_rows * soft[:, lanes] + target_rows * picked[:, lanes].astype(f32)
        df[pl.ds(k, PEERS, stride=PITCH), :] = piece[0:PEERS, :]
        df[pl.ds(PIECES + k, PEERS, stride=PITCH), :] = piece[PEERS:TOK, :]
    vocab_sketch = scale * columns[0:RANK, :] + target * columns[RANK : 2 * RANK, :]
    grad_sketch = scale * columns[2 * RANK : 3 * RANK, :] + target * columns[3 * RANK : 4 * RANK, :]
    acts = jnp.broadcast_to(acts, (PEERS, LANES))
    for place, values in enumerate((vocab_sketch, grad_sketch, acts)):
        high = values.astype(bf16).astype(f32)
        df[pl.ds(2 * PIECES + 2 * place, PEERS, stride=PITCH), :] = high
        df[pl.ds(2 * PIECES + 2 * place + 1, PEERS, stride=PITCH), :] = values - high
    for row in (6, 7):
        df[pl.ds(2 * PIECES + row, PEERS, stride=PITCH), :] = jnp.zeros((PEERS, LANES), f32)
    blocks[...] = df[...].reshape(PEERS, PITCH, LANES).astype(bf16)


def feature_kernel(blocks, aux, docs, core, mine, other, rows):
    rows[...] = blocks[...].astype(f32)[:, 2 * PIECES :, :].reshape(PEERS * 8, LANES)

    def row(place):
        return rows[pl.ds(place, PEERS, stride=8), :]

    vocab_column = jnp.sum(row(0) + row(1), axis=0, keepdims=True)
    grad_column = jnp.sum(row(2) + row(3), axis=0, keepdims=True)
    acts = row(4) + row(5)
    act_sketch = jnp.concatenate([acts[:, 0:RANK], acts[:, RANK : 2 * RANK]], axis=0)
    act_sketch = act_sketch * (RANK / FF) ** 0.5
    ids = lax.broadcasted_iota(jnp.int32, (DOCS, LANES), 0)
    member = (docs[0:1, :] == ids).astype(f32)
    high = lax.Precision.HIGHEST
    head = dot(member * vocab_column, aux[...], NT, high)
    down = dot(member * grad_column, act_sketch, NN, high)
    both = jnp.concatenate([head, down], axis=0)
    first, second = both[:, 0 : RANK // 2], both[:, RANK // 2 :]
    is_first = core[0:1, 0:1] == 0
    mine[...] = jnp.where(is_first, first, second)
    other[...] = jnp.where(is_first, second, first)


def resid_kernel(blocks, hidden, gain, out):
    received = blocks[...].astype(f32)
    total = jnp.zeros((2 * PIECES, LANES), f32)
    for source in range(PEERS):
        total = total + received[source, 0 : 2 * PIECES, :]
    grads = []
    for token in range(2):
        rows = slice(token * PIECES, (token + 1) * PIECES)
        values = hidden[rows, :].astype(f32)
        inv = lax.rsqrt(jnp.sum(values * values, keepdims=True) * (1.0 / D) + 1e-05)
        unit = values * inv
        weighted = gain[...] * total[rows, :]
        inner = jnp.sum(weighted * unit, keepdims=True) * (1.0 / D)
        grads.append(inv * (weighted - unit * inner))
    for k in range(PIECES):
        pair = jnp.concatenate([grads[0][k : k + 1, :], grads[1][k : k + 1, :]], axis=0)
        out[:, k * LANES : (k + 1) * LANES] = pair.astype(bf16)


def shards(
    hidden,
    norm_gain,
    head_weight,
    gate_up,
    targets,
    doc_ids,
    vocab_codes,
    hidden_codes,
    model_codes,
):
    index = lax.axis_index("tensor")
    core = lax.rem(index, 2)
    groups = [list(range(0, 2 * PEERS, 2)), list(range(1, 2 * PEERS, 2))]
    partner = [(i, i ^ 1) for i in range(2 * PEERS)]
    gain32 = norm_gain.astype(f32)
    gain_row = gain32.reshape(1, D)
    gain_blk = gain32.reshape(PIECES, LANES)
    own_rows = hidden.reshape(2 * PIECES, LANES)

    def exchange(rows):
        return lax.all_to_all(rows, "tensor", 0, 0, axis_index_groups=groups, tiled=True)

    with jax.named_scope("gather_hidden"):
        spread = call(
            spread_kernel,
            jax.ShapeDtypeStruct((PEERS, 2 * PIECES, LANES), bf16),
            [],
            1,
            1000,
            MIB,
        )(hidden)
        gathered = exchange(spread).reshape(PEERS * 2 * PIECES, LANES)
    with jax.named_scope("partner_rows"):
        size = VOC // PARTS
        w_par = [
            lax.ppermute(head_weight[part * size : (part + 1) * size], "tensor", partner)
            for part in range(PARTS)
        ]
    with jax.named_scope("activations"):
        act_part = call(act_kernel, jax.ShapeDtypeStruct((RANK, 256), f32), [], 2, 8000000, 300000)(
            gate_up, hidden_codes.reshape(1, -1)
        )
        act_part = act_part.T.reshape(PEERS, 2, LANES)
        act_mine = lax.dynamic_index_in_dim(act_part, core, axis=1, keepdims=False)
        act_other = lax.dynamic_index_in_dim(act_part, 1 - core, axis=1, keepdims=False)
        codes_own = vocab_codes.astype(f32).reshape(VOC // LANES, LANES)
        sent = jnp.concatenate([act_other, codes_own], axis=0)
        came = lax.ppermute(sent, "tensor", partner)
        acts = act_mine + came[:PEERS]
        codes_par = came[PEERS:].astype(jnp.int32).reshape(1, VOC)
        codes = jnp.concatenate([vocab_codes.reshape(1, VOC), codes_par], axis=1)
    with jax.named_scope("tables"):
        table = call(
            table_kernel, jax.ShapeDtypeStruct((3 * RANK, D), bf16), [], 2, 4000000, 1600000
        )(model_codes, gain_row)
        ids = jnp.stack([targets, doc_ids]).reshape(2, PEERS, 2, 2)
        ids = lax.dynamic_index_in_dim(ids, core, axis=2, keepdims=False)
        ids = ids.transpose(0, 2, 1).reshape(2, TOK)
        relative = ids[0] - index * VOC
        relative_par = ids[0] - (index + 1 - 2 * core) * VOC
        hit = jnp.where(
            (relative >= 0) & (relative < VOC),
            relative,
            jnp.where((relative_par >= 0) & (relative_par < VOC), relative_par + VOC, -1),
        ).reshape(1, TOK)
        docs = ids[1].reshape(1, TOK)
        core_row = jnp.full((1, LANES), core, jnp.int32)

    norm_scratch = [
        pltpu.VMEM((PEERS * PITCH, LANES), f32),
        pltpu.VMEM((TOK, D), bf16),
        pltpu.VMEM((TOK, D), bf16),
    ]
    with jax.named_scope("scores"):
        logits, payload = call(
            score_kernel,
            (
                jax.ShapeDtypeStruct((2 * VOC, TOK), f32),
                jax.ShapeDtypeStruct((PEERS * 4, LANES), f32),
            ),
            norm_scratch + [pltpu.VMEM((2 * VOC, D), bf16), pltpu.SemaphoreType.DMA((PARTS + 1,))],
            4 + PARTS,
            1 << 30,
            10 * MIB,
            any_inputs=range(3, 4 + PARTS),
        )(gathered, gain_blk, acts, head_weight, *w_par)
    with jax.named_scope("statistics"):
        stats = exchange(payload.reshape(PEERS, 4, LANES)).reshape(PEERS * 4, LANES)
    with jax.named_scope("backward"):
        soft, picked, columns, aux = call(
            backward_kernel,
            (
                jax.ShapeDtypeStruct((TOK, D), f32),
                jax.ShapeDtypeStruct((TOK, D), bf16),
                jax.ShapeDtypeStruct((4 * RANK + 16, LANES), f32),
                jax.ShapeDtypeStruct((RANK, LANES), f32),
            ),
            norm_scratch
            + [
                pltpu.VMEM((2 * VOC, D), bf16),
                pltpu.VMEM((TOK, D), f32),
                pltpu.VMEM((TOK, D), bf16),
                pltpu.SemaphoreType.DMA((D // CHUNK, PARTS + 1)),
                pltpu.SemaphoreType.DMA((D // CHUNK, 2)),
            ],
            7 + PARTS,
            3 << 30,
            12 * MIB,
            any_inputs=range(6, 7 + PARTS),
            any_outs=(0, 1),
        )(logits, hit, codes, table, gathered, gain_blk, head_weight, *w_par)
    with jax.named_scope("scale"):
        blocks = call(
            scale_kernel,
            jax.ShapeDtypeStruct((PEERS, PITCH, LANES), bf16),
            [
                pltpu.VMEM((PEERS * PITCH, LANES), f32),
                pltpu.VMEM((TOK, D), f32),
                pltpu.VMEM((TOK, D), bf16),
                pltpu.SemaphoreType.DMA((D // CHUNK, 2)),
            ],
            4,
            2000000,
            4 * MIB,
            any_inputs=(1, 2),
        )(stats, soft, picked, columns)
    with jax.named_scope("scatter_dnormed"):
        blocks, docs, core_row, gain_blk, aux, own_rows = lax.optimization_barrier(
            (blocks, docs, core_row, gain_blk, aux, own_rows)
        )
        received = exchange(blocks)
    with jax.named_scope("features"):
        half = jax.ShapeDtypeStruct((2 * DOCS, RANK // 2), f32)
        mine, other = call(
            feature_kernel,
            (half, half),
            [pltpu.VMEM((PEERS * 8, LANES), f32)],
            4,
            2000000,
            300000,
        )(received, aux, docs, core_row)
        features = mine + lax.ppermute(other, "tensor", partner)
    with jax.named_scope("resid_grad"):
        resid = call(
            resid_kernel,
            jax.ShapeDtypeStruct((2, D), bf16),
            [],
            3,
            2000000,
            MIB,
        )(received, own_rows, gain_blk)
    return resid, features[:DOCS], features[DOCS:]


def solution(mesh):
    in_specs = (
        P(("dp", "tensor"), None),
        P(),
        P("tensor", None),
        P(None, "tensor", "dp"),
        P("dp"),
        P("dp"),
        P("tensor"),
        P("tensor"),
        P(),
    )
    out_specs = (P(("dp", "tensor"), None), P("dp", "tensor"), P("dp", "tensor"))
    return jax.shard_map(shards, mesh=mesh, in_specs=in_specs, out_specs=out_specs, check_vma=False)
```
